32 devices in a mesh: batch: 8 (over y, x, core), seq: 4 (over z).
Axes of the slice: x: 2, y: 2, z: 4, core: 2. Of those that a mesh axis runs over, the one named last changes fastest.
Arguments:
- hidden_in: bfloat16 [8, 2048, 768], P('batch', 'seq'), may hold values from -6 to 6
- document_ids: int32 [8, 2048], P('batch', 'seq'), may hold values from 0 to 1018, as said below
- query_weight: bfloat16 [768, 768], replicated, may hold values from -0.21875 to 0.21875
- query_bias: float32 [768], replicated, may hold values from -3 to 3
- key_weight: bfloat16 [768, 768], replicated, may hold values from -0.21875 to 0.21875
- value_weight: bfloat16 [768, 768], replicated, may hold values from -0.21875 to 0.21875
- value_bias: float32 [768], replicated, may hold values from -3 to 3
- proj_weight: bfloat16 [768, 768], replicated, may hold values from -0.875 to 0.875
- proj_bias: float32 [768], replicated, may hold values from -3 to 3
- first_gain: float32 [768], replicated, may hold values from 0.5 to 1.5
- first_shift: float32 [768], replicated, may hold values from -3 to 3
- inner_weight: bfloat16 [768, 3072], replicated, may hold values from -0.21875 to 0.21875
- inner_bias: float32 [3072], replicated, may hold values from -3 to 3
- outer_weight: bfloat16 [3072, 768], replicated, may hold values from -0.109375 to 0.109375
- outer_bias: float32 [768], replicated, may hold values from -3 to 3
- second_gain: float32 [768], replicated, may hold values from 0.5 to 1.5
- second_shift: float32 [768], replicated, may hold values from -3 to 3
- output_grad: bfloat16 [8, 2048, 768], P('batch', 'seq'), may hold values from -6 to 6
Outputs:
- output: bfloat16 [8, 2048, 768], P('batch', 'seq')
- grad_hidden: bfloat16 [8, 2048, 768], P('batch', 'seq')
- grad_query_weight: float32 [768, 768], replicated
- grad_query_bias: float32 [768], replicated
- grad_key_weight: float32 [768, 768], replicated
- grad_value_weight: float32 [768, 768], replicated
- grad_value_bias: float32 [768], replicated
- grad_proj_weight: float32 [768, 768], replicated
- grad_proj_bias: float32 [768], replicated
- grad_first_gain: float32 [768], replicated
- grad_first_shift: float32 [768], replicated
- grad_inner_weight: float32 [768, 3072], replicated
- grad_inner_bias: float32 [3072], replicated
- grad_outer_weight: float32 [3072, 768], replicated
- grad_outer_bias: float32 [768], replicated
- grad_second_gain: float32 [768], replicated
- grad_second_shift: float32 [768], replicated
The draws below stay inside these ranges and needn't reach their ends.
Inputs may be any that keep to these rules, and one draw needn't show every extreme that they name: `document_ids`: along each row of 2048 positions the ids never fall and equal ids stand on consecutive positions. Each row holds one document that begins among its first 512 positions and ends among its last 512; every other document holds at most 512 positions.
All inputs are finite; a program needn't handle non-finite values.
Results may differ from the reference program's by a relative error of at most 0.015.
Values may be sent and summed in bfloat16 or wider, within the bound.
No kernel may reach another device: no remote copies, remote signals or barrier semaphores. Data moves between devices by JAX's collectives and lax.ppermute only.
A program may use at most 192 MiB of HBM per device.

```python
from functools import partial
import jax
import jax.numpy as jnp
from jax import lax

D = 768
HEADS = 12
HEAD_DIM = 64
FF = 3072
BLOCK = 512
SEQ_LEN = 2048
ROWS = 8


def draw_document_ids(key, part):
    key = jax.random.fold_in(key, 5)
    key_begin, key_finish, key_front, key_back = jax.random.split(key, 4)
    position = jnp.arange(SEQ_LEN, dtype=jnp.int32)
    begin = jax.random.randint(key_begin, (ROWS, 1), 0, BLOCK)
    finish = SEQ_LEN - jax.random.randint(key_finish, (ROWS, 1), 1, BLOCK)
    front_lengths = jax.random.randint(key_front, (ROWS, 72), 30, 513)
    back_lengths = jax.random.randint(key_back, (ROWS, 72), 30, 513)
    front_bounds = jnp.cumsum(front_lengths, axis=1)
    back_bounds = jnp.cumsum(back_lengths, axis=1)
    front_count = jnp.sum((front_bounds[:, None, :] <= position[None, :, None]).astype(jnp.int32), axis=2)
    offset = position[None, :] - finish
    back_count = jnp.sum((back_bounds[:, None, :] <= offset[:, :, None]).astype(jnp.int32), axis=2)
    middle = jnp.where(position[None, :] < finish, 1000, 1001 + back_count)
    return jnp.where(position[None, :] < begin, front_count, middle).astype(jnp.int32)


def level_of(stream_key, shape, cuts, least, high):
    level = 1.0
    for dim, shards_of in cuts:
        draws = jax.random.uniform(jax.random.fold_in(jax.random.fold_in(stream_key, 6), dim), (shards_of,), jnp.float32, least / len(cuts), high / len(cuts))
        level = level * jnp.repeat(jnp.exp(draws), shape[dim] // shards_of).reshape((-1,) + (1,) * (len(shape) - 1 - dim))
    return level


def centred(stream_key, dims, spread, reach, shards=(), held_as=jnp.bfloat16):
    values = jax.random.normal(stream_key, dims, jnp.float32) * spread
    if len(shards) > 0:
        values = level_of(stream_key, dims, shards, -0.22, 0.18) * values
    return jnp.clip(values, min=-reach, max=reach).astype(held_as)


def setup_inputs(seed: int = 0) -> dict:
    splits = jax.random.split(jax.random.key(seed), 19)
    hidden_in = centred(splits[0], (ROWS, SEQ_LEN, D), 1.0, 6.0, ((0, 8), (1, 4)))
    document_ids = draw_document_ids(jax.random.fold_in(splits[18], 71), 0)
    query_weight = centred(splits[2], (D, D), D ** -0.5, 0.21875)
    query_bias = centred(splits[3], (D,), 0.5, 3.0, (), jnp.float32)
    key_weight = centred(splits[4], (D, D), D ** -0.5, 0.21875)
    value_weight = centred(splits[5], (D, D), D ** -0.5, 0.21875)
    value_bias = centred(splits[6], (D,), 0.5, 3.0, (), jnp.float32)
    proj_weight = centred(splits[7], (D, D), (D // 16) ** -0.5, 0.875)
    proj_bias = centred(splits[8], (D,), 0.5, 3.0, (), jnp.float32)
    first_gain = jnp.clip(1.0 + 0.1 * jax.random.normal(splits[9], (D,), jnp.float32), 0.5, 1.5)
    first_shift = centred(splits[10], (D,), 0.5, 3.0, (), jnp.float32)
    inner_weight = centred(splits[11], (D, FF), D ** -0.5, 0.21875)
    inner_bias = centred(splits[12], (FF,), 0.5, 3.0, (), jnp.float32)
    outer_weight = centred(splits[13], (FF, D), FF ** -0.5, 0.109375)
    outer_bias = centred(splits[14], (D,), 0.5, 3.0, (), jnp.float32)
    second_gain = jnp.clip(1.0 + 0.1 * jax.random.normal(splits[15], (D,), jnp.float32), 0.5, 1.5)
    second_shift = centred(splits[16], (D,), 0.5, 3.0, (), jnp.float32)
    output_grad = centred(splits[17], (ROWS, SEQ_LEN, D), 1.0, 6.0, ((0, 8), (1, 4)))
    return dict(hidden_in=hidden_in, document_ids=document_ids, query_weight=query_weight, query_bias=query_bias, key_weight=key_weight, value_weight=value_weight, value_bias=value_bias, proj_weight=proj_weight, proj_bias=proj_bias, first_gain=first_gain, first_shift=first_shift, inner_weight=inner_weight, inner_bias=inner_bias, outer_weight=outer_weight, outer_bias=outer_bias, second_gain=second_gain, second_shift=second_shift, output_grad=output_grad)


@jax.custom_vjp
def low(v):
    return lax.optimization_barrier(v.astype(jnp.bfloat16)).astype(jnp.float32)

@jax.custom_vjp
def low_back(v):
    return v

def low_keep(v):
    return (low(v), None)

def low_pass(kept, grad):
    return (grad,)

def back_keep(v):
    return (v, None)

def back_low(kept, grad):
    return (low(grad),)
low.defvjp(low_keep, low_pass)
low_back.defvjp(back_keep, back_low)
EPSILON = 1e-05

def product(left, right):
    return jnp.dot(left, right, precision=lax.Precision.HIGHEST, preferred_element_type=jnp.float32)

def layer_norm(values, gain, shift):
    center = values - lax.optimization_barrier(jnp.mean(values, axis=-1, keepdims=True))
    inverse = lax.rsqrt(lax.optimization_barrier(jnp.mean(center * center, axis=-1, keepdims=True)) + EPSILON)
    return center * inverse * gain + shift

def head_attend(same_doc, operands):
    query_head, key_head, value_head = operands
    scores = low_back(product(query_head, key_head.T) * HEAD_DIM ** (-0.5))
    scores = jnp.where(same_doc, scores, -1e+30)
    row_peak = lax.optimization_barrier(jnp.max(scores, axis=-1, keepdims=True))
    log_total = row_peak + jnp.log(lax.optimization_barrier(jnp.sum(jnp.exp(scores - row_peak), axis=-1, keepdims=True)))
    attn_prob = low(jnp.exp(scores - log_total))
    return product(attn_prob, value_head)

def split_heads(values):
    return values.reshape(values.shape[0], HEADS, HEAD_DIM).transpose(1, 0, 2)

def encoder_row(hidden, same_doc, params):
    query_weight, query_bias, key_weight, value_weight, value_bias, proj_weight, proj_bias, first_gain, first_shift, inner_weight, inner_bias, outer_weight, outer_bias, second_gain, second_shift = params
    queries = low(low_back(product(hidden, query_weight) + query_bias))
    key_rows = low(low_back(product(hidden, key_weight)))
    value_rows = low(low_back(product(hidden, value_weight) + value_bias))
    attended = lax.map(jax.checkpoint(partial(head_attend, same_doc)), (split_heads(queries), split_heads(key_rows), split_heads(value_rows)))
    attended = low(low_back(attended.transpose(1, 0, 2).reshape(hidden.shape[0], D)))
    branch = low_back(product(attended, proj_weight) + proj_bias)
    first = layer_norm(hidden + branch, first_gain, first_shift)
    inner_act = low_back(product(low(first), inner_weight) + inner_bias)
    activated = low(jax.nn.gelu(inner_act, approximate=False))
    outer_act = low_back(product(activated, outer_weight) + outer_bias)
    return layer_norm(first + outer_act, second_gain, second_shift)

def reference(hidden_in, document_ids, query_weight, query_bias, key_weight, value_weight, value_bias, proj_weight, proj_bias, first_gain, first_shift, inner_weight, inner_bias, outer_weight, outer_bias, second_gain, second_shift, output_grad):
    params = tuple((weight.astype(jnp.float32) for weight in (query_weight, query_bias, key_weight, value_weight, value_bias, proj_weight, proj_bias, first_gain, first_shift, inner_weight, inner_bias, outer_weight, outer_bias, second_gain, second_shift)))

    def one_row(totals, packed):
        hidden_row, ids_row, grad_row = packed
        same_doc = ids_row[:, None] == ids_row[None, :]

        def forward(hidden_value, weights):
            return encoder_row(hidden_value, same_doc, weights)
        result, pullback = jax.vjp(forward, hidden_row.astype(jnp.float32), params)
        grad_input, grad_params = pullback(grad_row.astype(jnp.float32))
        totals = tuple((total + term for total, term in zip(totals, grad_params)))
        return (totals, (result.astype(jnp.bfloat16), grad_input.astype(jnp.bfloat16)))
    zeros = tuple((jnp.zeros(weight.shape, jnp.float32) for weight in params))
    totals, (outputs, grad_hidden) = lax.scan(one_row, zeros, (hidden_in, document_ids, output_grad))
    return (outputs, grad_hidden, totals[0], totals[1], totals[2], totals[3], totals[4], totals[5], totals[6], totals[7], totals[8], totals[9], totals[10], totals[11], totals[12], totals[13], totals[14])
```

```python
import functools
import jax
import jax.numpy as jnp
from jax import lax
from jax.experimental import pallas as pl
from jax.experimental.pallas import tpu as pltpu
from jax.sharding import PartitionSpec as P

HEAD_DIM = 64
PAIR = 128
MASKED = -1e30

NT = (((1,), (1,)), ((), ()))
NN = (((1,), (0,)), ((), ()))


def dot(left, right, dims):
    return lax.dot_general(left, right, dims, preferred_element_type=jnp.float32)


def lane_half(x, half):
    lanes = lax.broadcasted_iota(jnp.int32, x.shape, 1)
    keep = lanes < HEAD_DIM if half == 0 else lanes >= HEAD_DIM
    return jnp.where(keep, x, jnp.zeros_like(x))


def fill_bias(bias_ref, kind_ref, ids_q_ref, ids_k_ref, slots, block):
    for slot in range(slots):

        @pl.when(kind_ref[slot] == 2)
        def _():
            same = ids_k_ref[pl.ds(slot * block, block), :] == ids_q_ref[...]
            bias_ref[slot] = jnp.where(same, 0.0, MASKED)


def forward_kernel(
    slots, block, first, kind_ref, q_ref, k_ref, v_ref, ids_q_ref, ids_k_ref, *refs
):
    if first:
        acc_out, peak_out, sum_out, bias_ref = refs
        acc_out[...] = jnp.zeros_like(acc_out)
        sum_out[...] = jnp.zeros_like(sum_out)
        peak_out[...] = jnp.full(peak_out.shape, MASKED, jnp.float32)
    else:
        acc_in, peak_in, sum_in, acc_out, peak_out, sum_out, bias_ref = refs
        acc_out[...] = acc_in[...]
        sum_out[...] = sum_in[...]
        peak_out[...] = peak_in[...]

    @pl.when(pl.program_id(0) == 0)
    def _():
        fill_bias(bias_ref, kind_ref, ids_q_ref, ids_k_ref, slots, block)

    q = q_ref[...]
    ones = jnp.ones((16, block), jnp.bfloat16)
    for slot in range(slots):

        def visit(masked):
            k = k_ref[pl.ds(slot * block, block), :]
            v_t = v_ref[pl.ds(slot * block, block), :].T
            scores = [dot(k, lane_half(q, half), NT) for half in range(2)]
            if masked:
                scores = [x + bias_ref[slot] for x in scores]
            old = [peak_out[0, half : half + 1, :] for half in range(2)]
            peak = [jnp.maximum(o, jnp.max(x, axis=0, keepdims=True)) for o, x in zip(old, scores)]
            prob = [jnp.exp(x - m).astype(jnp.bfloat16) for x, m in zip(scores, peak)]
            for half in range(2):
                shrink = jnp.exp(old[half] - peak[half])
                rows = slice(half * HEAD_DIM, (half + 1) * HEAD_DIM)
                mixed = dot(jnp.concatenate([v_t[rows], ones], axis=0), prob[half], NN)
                acc_out[rows, :] = acc_out[rows, :] * shrink + mixed[:HEAD_DIM]
                sum_out[0, half : half + 1, :] = (
                    sum_out[0, half : half + 1, :] * shrink + mixed[HEAD_DIM : HEAD_DIM + 1]
                )
                peak_out[0, half : half + 1, :] = peak[half]

        pl.when(kind_ref[slot] == 1)(functools.partial(visit, False))
        pl.when(kind_ref[slot] == 2)(functools.partial(visit, True))


def attend_forward(kinds, q, k, v, ids_q, ids_k, state):
    block, width = q.shape
    slots = k.shape[0] // block
    pairs = width // PAIR
    rows = pl.BlockSpec((1, 2, block), lambda p, kinds: (p, 0, 0))
    acc = pl.BlockSpec((PAIR, block), lambda p, kinds: (p, 0))
    state_specs = [acc, rows, rows]
    in_specs = [
        pl.BlockSpec((block, PAIR), lambda p, kinds: (0, p)),
        pl.BlockSpec((slots * block, PAIR), lambda p, kinds: (0, p)),
        pl.BlockSpec((slots * block, PAIR), lambda p, kinds: (0, p)),
        pl.BlockSpec((1, block), lambda p, kinds: (0, 0)),
        pl.BlockSpec((slots * block, 1), lambda p, kinds: (0, 0)),
    ]
    out_shape = [
        jax.ShapeDtypeStruct((width, block), jnp.float32),
        jax.ShapeDtypeStruct((pairs, 2, block), jnp.float32),
        jax.ShapeDtypeStruct((pairs, 2, block), jnp.float32),
    ]
    first = state is None
    return pl.pallas_call(
        functools.partial(forward_kernel, slots, block, first),
        grid_spec=pltpu.PrefetchScalarGridSpec(
            num_scalar_prefetch=1,
            grid=(pairs,),
            in_specs=in_specs + ([] if first else state_specs),
            out_specs=state_specs,
            scratch_shapes=[pltpu.VMEM((slots, block, block), jnp.float32)],
        ),
        out_shape=out_shape,
        compiler_params=pltpu.CompilerParams(vmem_limit_bytes=48 * 2**20),
        cost_estimate=pl.CostEstimate(
            flops=int(4 * slots * block * block * width * 2),
            bytes_accessed=int(4 * slots * block * width + 8 * block * width),
            transcendentals=0,
        ),
        name="attend_forward",
    )(kinds, q, k, v, ids_q, ids_k, *([] if first else state))


def backward_kernel(
    slots, block, first, kind_ref, q_ref, g_ref, k_ref, v_ref, total_ref, delta_ref, ids_q_ref, ids_k_ref, *refs
):
    if first:
        grad_q, grad_k, grad_v, bias_ref = refs
        grad_q[...] = jnp.zeros_like(grad_q)
    else:
        grad_q_in, grad_q, grad_k, grad_v, bias_ref = refs
        grad_q[...] = grad_q_in[...]

    @pl.when(pl.program_id(0) == 0)
    def _():
        fill_bias(bias_ref, kind_ref, ids_q_ref, ids_k_ref, slots, block)

    q, g = q_ref[...], g_ref[...]
    for slot in range(slots):
        here = pl.ds(slot * block, block)

        def visit(masked):
            k, v = k_ref[here, :], v_ref[here, :]
            k_t = k.T
            sum_k = sum_v = None
            for half in range(2):
                q_half, g_half = lane_half(q, half), lane_half(g, half)
                scores = dot(k, q_half, NT)
                if masked:
                    scores = scores + bias_ref[slot]
                prob = jnp.exp(scores - total_ref[0, half : half + 1, :])
                grad_prob = dot(v, g_half, NT)
                grad_score = (prob * (grad_prob - delta_ref[0, half : half + 1, :])).astype(jnp.bfloat16)
                part_v = dot(prob.astype(jnp.bfloat16), g_half, NN)
                part_k = dot(grad_score, q_half, NN)
                sum_v = part_v if sum_v is None else sum_v + part_v
                sum_k = part_k if sum_k is None else sum_k + part_k
                rows = slice(half * HEAD_DIM, (half + 1) * HEAD_DIM)
                grad_q[rows, :] += dot(k_t[rows], grad_score, NN)
            grad_k[here, :] = sum_k.astype(jnp.bfloat16)
            grad_v[here, :] = sum_v.astype(jnp.bfloat16)

        pl.when(kind_ref[slot] == 1)(functools.partial(visit, False))
        pl.when(kind_ref[slot] == 2)(functools.partial(visit, True))

        @pl.when(kind_ref[slot] == 0)
        def _():
            grad_k[here, :] = jnp.zeros((block, PAIR), jnp.bfloat16)
            grad_v[here, :] = jnp.zeros((block, PAIR), jnp.bfloat16)


def attend_backward(kinds, q, g, k, v, totals, deltas, ids_q, ids_k, grad_q):
    block, width = q.shape
    slots = k.shape[0] // block
    pairs = width // PAIR
    rows = pl.BlockSpec((1, 2, block), lambda p, kinds: (p, 0, 0))
    acc = pl.BlockSpec((PAIR, block), lambda p, kinds: (p, 0))
    mine = pl.BlockSpec((block, PAIR), lambda p, kinds: (0, p))
    theirs = pl.BlockSpec((slots * block, PAIR), lambda p, kinds: (0, p))
    first = grad_q is None
    return pl.pallas_call(
        functools.partial(backward_kernel, slots, block, first),
        grid_spec=pltpu.PrefetchScalarGridSpec(
            num_scalar_prefetch=1,
            grid=(pairs,),
            in_specs=[mine, mine, theirs, theirs, rows, rows]
            + [
                pl.BlockSpec((1, block), lambda p, kinds: (0, 0)),
                pl.BlockSpec((slots * block, 1), lambda p, kinds: (0, 0)),
            ]
            + ([] if first else [acc]),
            out_specs=[acc, theirs, theirs],
            scratch_shapes=[pltpu.VMEM((slots, block, block), jnp.float32)],
        ),
        out_shape=[
            jax.ShapeDtypeStruct((width, block), jnp.float32),
            jax.ShapeDtypeStruct((slots * block, width), jnp.bfloat16),
            jax.ShapeDtypeStruct((slots * block, width), jnp.bfloat16),
        ],
        compiler_params=pltpu.CompilerParams(vmem_limit_bytes=48 * 2**20),
        cost_estimate=pl.CostEstimate(
            flops=int(10 * slots * block * block * width * 2),
            bytes_accessed=int(8 * slots * block * width + 12 * block * width),
            transcendentals=0,
        ),
        name="attend_backward",
    )(kinds, q, g, k, v, totals, deltas, ids_q, ids_k, *([] if first else [grad_q]))


EPSILON = 1e-05
ROOT_HALF = 0.7071067811865476
ROOT_TAU = 0.3989422804014327


def low(x):
    return x.astype(jnp.bfloat16)


def times(left, right):
    return dot(left, right, NN)


def times_back(left, right):
    return dot(left, right, NT)


def weight_grad(left, right):
    return dot(left, right, (((0,), (0,)), ((), ())))


def column_sums(x):
    return jnp.sum(x.astype(jnp.float32), axis=0)


def layer_norm(values, gain, shift):
    center = values - jnp.mean(values, axis=-1, keepdims=True)
    inverse = lax.rsqrt(jnp.mean(center * center, axis=-1, keepdims=True) + EPSILON)
    scaled = center * inverse
    return scaled * gain + shift, scaled, inverse


def norm_back(grad_out, scaled, inverse, gain):
    grad_scaled = grad_out * gain
    grad_in = inverse * (
        grad_scaled
        - jnp.mean(grad_scaled, axis=-1, keepdims=True)
        - scaled * jnp.mean(grad_scaled * scaled, axis=-1, keepdims=True)
    )
    return grad_in, jnp.sum(grad_out * scaled, axis=0), jnp.sum(grad_out, axis=0)


def swap(x, bit, count):
    return lax.ppermute(x, "batch", [(i, i ^ bit) for i in range(count)])


def pick(x, index, parts, axis):
    size = x.shape[axis] // parts
    return lax.dynamic_slice_in_dim(x, index * size, size, axis)


def add_low(left, right):
    return low(left.astype(jnp.float32) + right.astype(jnp.float32))


def halve(x, bit, count):
    side = (lax.axis_index("batch") // bit) % 2
    return add_low(pick(x, side, 2, 0), swap(pick(x, 1 - side, 2, 0), bit, count))


def unhalve(x, bit, count):
    side = (lax.axis_index("batch") // bit) % 2
    other = swap(x, bit, count)
    return jnp.where(
        side == 0, jnp.concatenate([x, other], axis=0), jnp.concatenate([other, x], axis=0)
    )


def turn(x, distance, count):
    return lax.ppermute(x, "seq", [(i, (i + distance) % count) for i in range(count)])


def reduce_all(x, batch, seq):
    bits = [1 << i for i in range(batch.bit_length() - 1)]
    rest = bits[1:]
    orders = (rest, rest[::-1])
    half = halve(x, 1, batch)
    sides = list(jnp.split(half, 2, axis=0))
    for step in range(len(rest)):
        sides = [halve(side, order[step], batch) for side, order in zip(sides, orders)]
    held = jnp.concatenate(sides, axis=1)
    me = lax.axis_index("seq")
    total = pick(held, me, seq, 1).astype(jnp.float32)
    for distance in range(1, seq):
        total += turn(pick(held, (me + distance) % seq, seq, 1), distance, seq).astype(jnp.float32)
    mine = low(total)
    around = [mine] + [turn(mine, seq - step, seq) for step in range(1, seq)]
    width = mine.shape[1]
    ahead = jnp.concatenate(around + around, axis=1)
    held = lax.dynamic_slice_in_dim(ahead, ((seq - me) % seq) * width, seq * width, 1)
    sides = list(jnp.split(held, 2, axis=1))
    for step in reversed(range(len(rest))):
        sides = [unhalve(side, order[step], batch) for side, order in zip(sides, orders)]
    return unhalve(jnp.concatenate(sides, axis=0), 1, batch).astype(jnp.float32)


def reduce_small(x, batch, seq):
    for i in range(batch.bit_length() - 1):
        x = x + swap(x, 1 << i, batch)
    return x + sum(turn(x, distance, seq) for distance in range(1, seq))


def kind_of(valid, ids_q, ids_k):
    apart = (ids_q[-1] < ids_k[0]) | (ids_k[-1] < ids_q[0])
    one = (ids_q[0] == ids_k[-1]) & (ids_q[-1] == ids_k[0])
    return jnp.where(jnp.logical_not(valid) | apart, 0, jnp.where(one, 1, 2)).astype(jnp.int32)


def shards(
    batch,
    seq,
    hidden_in,
    document_ids,
    query_weight,
    query_bias,
    key_weight,
    value_weight,
    value_bias,
    proj_weight,
    proj_bias,
    first_gain,
    first_shift,
    inner_weight,
    inner_bias,
    outer_weight,
    outer_bias,
    second_gain,
    second_shift,
    output_grad,
):
    hidden = hidden_in[0]
    ids = document_ids[0]
    grad_out = output_grad[0].astype(jnp.float32)
    block, width = hidden.shape
    heads = width // HEAD_DIM
    me = lax.axis_index("seq")
    scale = HEAD_DIM ** (-0.5)

    steps = []
    left, right = (hidden, ids), (hidden, ids)
    for s in range(1, seq):
        to_right = [(i, i + 1) for i in range(s - 1, seq - 1)]
        to_left = [(i, i - 1) for i in range(1, seq - s + 1)]
        left = tuple(lax.ppermute(x, "seq", to_right) for x in left)
        right = tuple(lax.ppermute(x, "seq", to_left) for x in right)
        has_left, has_right = me >= s, me + s <= seq - 1
        if 2 * s <= seq - 1:
            slots = [(has_left,) + left, (has_right,) + right]
        else:
            slots = [
                (has_left | has_right,)
                + tuple(jnp.where(has_left, a, b) for a, b in zip(left, right))
            ]
        steps.append(slots)
    groups = [[(me >= 0, hidden, ids)]] + steps

    queries = low((times(hidden, query_weight) + query_bias)) * jnp.bfloat16(scale)
    ids_q = ids[None, :]
    state = None
    kept = []
    for slots in groups:
        tokens = jnp.concatenate([slot[1] for slot in slots], axis=0)
        ids_k = jnp.concatenate([slot[2] for slot in slots], axis=0)
        kinds = jnp.stack([kind_of(slot[0], ids, slot[2]) for slot in slots])
        keys = low(times(tokens, key_weight))
        values = low(times(tokens, value_weight) + value_bias)
        state = attend_forward(kinds, queries, keys, values, ids_q, ids_k[:, None], state)
        kept.append((kinds, tokens, keys, values, ids_k[:, None]))
    acc, peak, sums = state
    attended_t = acc.reshape(heads, HEAD_DIM, block) / sums.reshape(heads, 1, block)
    attended_full = attended_t.reshape(width, block).T
    attended = low(attended_full)
    totals = peak + jnp.log(sums)

    branch = times(attended, proj_weight) + proj_bias
    first, first_scaled, first_inverse = layer_norm(
        hidden.astype(jnp.float32) + branch, first_gain, first_shift
    )
    first_low = low(first)
    inner_act = times(first_low, inner_weight) + inner_bias
    chance = 0.5 * (1.0 + lax.erf(inner_act * ROOT_HALF))
    activated = low(inner_act * chance)
    slope = chance + inner_act * (ROOT_TAU * jnp.exp(-0.5 * inner_act * inner_act))
    outer_act = times(activated, outer_weight) + outer_bias
    second, second_scaled, second_inverse = layer_norm(first + outer_act, second_gain, second_shift)
    result = low(second)
    grad_mix, grad_second_gain, grad_second_shift = norm_back(
        grad_out, second_scaled, second_inverse, second_gain
    )
    grad_outer = low(grad_mix)
    grad_outer_weight = reduce_all(low(weight_grad(activated, grad_outer)), batch, seq)
    grad_outer_bias = column_sums(grad_outer)
    grad_inner = low(times_back(grad_outer, outer_weight) * slope)
    grad_inner_bias = column_sums(grad_inner)
    grad_first = grad_mix + times_back(grad_inner, inner_weight)
    grad_resid, grad_first_gain, grad_first_shift = norm_back(
        grad_first, first_scaled, first_inverse, first_gain
    )
    grad_branch = low(grad_resid)
    grad_proj_bias = column_sums(grad_branch)
    early = reduce_all(
        jnp.concatenate(
            [low(weight_grad(first_low, grad_inner)), low(weight_grad(attended, grad_branch))], axis=1
        ),
        batch,
        seq,
    )
    grad_inner_weight, grad_proj_weight = jnp.split(early, [inner_weight.shape[1]], axis=1)
    grad_attended = low(times_back(grad_branch, proj_weight))
    deltas = jnp.sum(
        (grad_attended.astype(jnp.float32) * attended_full).reshape(block, heads, HEAD_DIM), axis=-1
    ).T.reshape(heads // 2, 2, block)

    grad_query_t = None
    grad_key_weight = grad_value_weight = grad_value_bias = 0.0
    to_left = to_right = None
    for s in reversed(range(seq)):
        kinds, tokens, keys, values, ids_k = kept[s]
        grad_query_t, grad_keys, grad_values = attend_backward(
            kinds, queries, grad_attended, keys, values, totals, deltas, ids_q, ids_k, grad_query_t
        )
        grad_key_weight += weight_grad(tokens, grad_keys)
        grad_value_weight += weight_grad(tokens, grad_values)
        grad_value_bias += column_sums(grad_values)
        terms = times_back(grad_keys, key_weight) + times_back(grad_values, value_weight)
        if s == 0:
            own_terms = terms
            break
        has_left, has_right = me >= s, me + s <= seq - 1
        if len(steps[s - 1]) == 2:
            left_terms, right_terms = jnp.split(terms, 2, axis=0)
        else:
            left_terms = jnp.where(has_left, terms, 0.0)
            right_terms = jnp.where(has_right, terms, 0.0)
        if to_left is not None:
            left_terms = left_terms + to_left.astype(jnp.float32)
            right_terms = right_terms + to_right.astype(jnp.float32)
        to_left = lax.ppermute(low(left_terms), "seq", [(i, i - 1) for i in range(s, seq)])
        to_right = lax.ppermute(low(right_terms), "seq", [(i, i + 1) for i in range(seq - s)])
    grad_queries = low(grad_query_t * scale).T
    grad_query_weight = weight_grad(hidden, grad_queries)
    grad_query_bias = column_sums(grad_queries)
    own_terms = own_terms + grad_resid + times_back(grad_queries, query_weight)
    if to_left is not None:
        own_terms = own_terms + to_left.astype(jnp.float32) + to_right.astype(jnp.float32)
    grad_input = low(own_terms)
    late = reduce_all(
        jnp.concatenate([low(grad_query_weight), low(grad_key_weight), low(grad_value_weight)], axis=1),
        batch,
        seq,
    )
    grad_query_weight, grad_key_weight, grad_value_weight = jnp.split(late, 3, axis=1)

    small = [
        grad_query_bias,
        grad_value_bias,
        grad_proj_bias,
        grad_first_gain,
        grad_first_shift,
        grad_outer_bias,
        grad_second_gain,
        grad_second_shift,
        grad_inner_bias,
    ]
    together = reduce_small(jnp.concatenate(small), batch, seq)
    sizes = [x.shape[0] for x in small]
    cuts = [sum(sizes[: i + 1]) for i in range(len(sizes) - 1)]
    (
        grad_query_bias,
        grad_value_bias,
        grad_proj_bias,
        grad_first_gain,
        grad_first_shift,
        grad_outer_bias,
        grad_second_gain,
        grad_second_shift,
        grad_inner_bias,
    ) = jnp.split(together, cuts)
    return (
        result[None],
        grad_input[None],
        grad_query_weight,
        grad_query_bias,
        grad_key_weight,
        grad_value_weight,
        grad_value_bias,
        grad_proj_weight,
        grad_proj_bias,
        grad_first_gain,
        grad_first_shift,
        grad_inner_weight,
        grad_inner_bias,
        grad_outer_weight,
        grad_outer_bias,
        grad_second_gain,
        grad_second_shift,
    )


def solution(mesh):
    rows = P("batch", "seq", None)
    return jax.shard_map(
        functools.partial(shards, mesh.shape["batch"], mesh.shape["seq"]),
        mesh=mesh,
        in_specs=(rows, P("batch", "seq")) + (P(),) * 15 + (rows,),
        out_specs=(rows, rows) + (P(),) * 15,
        check_vma=False,
    )
```

```python
import functools

import jax
import jax.numpy as jnp
from jax import lax
from jax.experimental import pallas as pl
from jax.experimental.pallas import tpu as pltpu
from jax.sharding import PartitionSpec as P

HEAD_DIM = 64
PAIR = 2 * HEAD_DIM
MASKED = -1e30
EPSILON = 1e-05
ROOT_HALF = 0.7071067811865476
ROOT_TAU = 0.3989422804014327
PHASES = 1
ID_BASE = 128

NT = (((1,), (1,)), ((), ()))
NN = (((1,), (0,)), ((), ()))
TN = (((0,), (0,)), ((), ()))


def dot(left, right, dims):
    return lax.dot_general(left, right, dims, preferred_element_type=jnp.float32)


def low(x):
    return x.astype(jnp.bfloat16)


def high(x):
    return x.astype(jnp.float32)


def times(left, right):
    return dot(left, right, NN)


def times_back(left, right):
    return dot(left, right, NT)


def weight_grad(left, right):
    return dot(left, right, TN)


def column_sums(x):
    return jnp.sum(high(x), axis=0)


def lane_half(x, half):
    lanes = lax.broadcasted_iota(jnp.int32, x.shape, 1)
    keep = lanes < HEAD_DIM if half == 0 else lanes >= HEAD_DIM
    return jnp.where(keep, x, jnp.zeros_like(x))


def head_rows(half):
    return slice(half * HEAD_DIM, (half + 1) * HEAD_DIM)


def look(kind_ref, bias_ref, ids_q_ref, ids_k_ref):
    @pl.when(pl.program_id(0) == 0)
    def _():
        ids_q, ids_k = ids_q_ref[...], ids_k_ref[...]
        low_q, high_q, low_k, high_k = jnp.min(ids_q), jnp.max(ids_q), jnp.min(ids_k), jnp.max(ids_k)
        apart = (high_q < low_k) | (high_k < low_q)
        one = (low_q == high_k) & (low_k == high_q)
        kind_ref[0] = jnp.where(apart, 0, jnp.where(one, 1, 2)).astype(jnp.int32)

        @pl.when(kind_ref[0] == 2)
        def _():
            bias_ref[...] = jnp.where(ids_k == ids_q, 0.0, MASKED)


def forward_kernel(first, last, q_ref, k_ref, v_ref, ids_q_ref, ids_k_ref, *refs):
    if first:
        acc_in = peak_in = sum_in = None
    else:
        acc_in, peak_in, sum_in = refs[:3]
        refs = refs[3:]
    if last:
        acc_out, total_out, attended_out, acc, peak, sums, kind_ref, bias_ref = refs
    else:
        acc, peak, sums, kind_ref, bias_ref = refs
    if first:
        acc[...] = jnp.zeros_like(acc)
        sums[...] = jnp.zeros_like(sums)
        peak[...] = jnp.full(peak.shape, MASKED, jnp.float32)
    else:
        acc[...] = acc_in[...]
        sums[...] = sum_in[...]
        peak[...] = peak_in[...]
    look(kind_ref, bias_ref, ids_q_ref, ids_k_ref)

    def visit(masked):
        q, k = q_ref[...], k_ref[...]
        v_t = v_ref[...].T
        ones = jnp.ones((16, k.shape[0]), jnp.bfloat16)
        scores = [dot(k, lane_half(q, half), NT) for half in range(2)]
        if masked:
            scores = [x + bias_ref[...] for x in scores]
        old = [peak[0, half : half + 1, :] for half in range(2)]
        new = [jnp.maximum(o, jnp.max(x, axis=0, keepdims=True)) for o, x in zip(old, scores)]
        prob = [low(jnp.exp(x - m)) for x, m in zip(scores, new)]
        for half in range(2):
            shrink = jnp.exp(old[half] - new[half])
            rows, one = head_rows(half), slice(half, half + 1)
            mixed = dot(jnp.concatenate([v_t[rows], ones], axis=0), prob[half], NN)
            acc[rows, :] = acc[rows, :] * shrink + mixed[:HEAD_DIM]
            sums[0, one, :] = sums[0, one, :] * shrink + mixed[HEAD_DIM : HEAD_DIM + 1]
            peak[0, one, :] = new[half]

    pl.when(kind_ref[0] == 1)(functools.partial(visit, False))
    pl.when(kind_ref[0] == 2)(functools.partial(visit, True))

    if last:
        for half in range(2):
            rows, one = head_rows(half), slice(half, half + 1)
            acc_out[rows, :] = acc[rows, :] / sums[0, one, :]
            total_out[0, one, :] = peak[0, one, :] + jnp.log(sums[0, one, :])
        attended_out[...] = low(acc_out[...].T)


def attend_forward(q, kv, ids_q, ids_k, state, last):
    block, width = q.shape
    pairs = width // PAIR
    first = state is None
    rows = pl.BlockSpec((1, 2, block), lambda p: (p, 0, 0))
    acc = pl.BlockSpec((PAIR, block), lambda p: (p, 0))
    mine = pl.BlockSpec((block, PAIR), lambda p: (0, p))
    acc_shape = jax.ShapeDtypeStruct((width, block), jnp.float32)
    row_shape = jax.ShapeDtypeStruct((pairs, 2, block), jnp.float32)
    scratch = [pltpu.SMEM((1,), jnp.int32), pltpu.VMEM((block, block), jnp.float32)]
    if last:
        out_specs = [acc, rows, mine]
        out_shape = [acc_shape, row_shape, jax.ShapeDtypeStruct((block, width), jnp.bfloat16)]
        scratch = [
            pltpu.VMEM((PAIR, block), jnp.float32),
            pltpu.VMEM((1, 2, block), jnp.float32),
            pltpu.VMEM((1, 2, block), jnp.float32),
        ] + scratch
    else:
        out_specs, out_shape = [acc, rows, rows], [acc_shape, row_shape, row_shape]
    return pl.pallas_call(
        functools.partial(forward_kernel, first, last),
        grid_spec=pl.GridSpec(
            grid=(pairs,),
            in_specs=[
                mine,
                mine,
                pl.BlockSpec((block, PAIR), lambda p: (0, p + pairs)),
                pl.BlockSpec((1, block), lambda p: (0, 0)),
                pl.BlockSpec((block, 1), lambda p: (0, 0)),
            ]
            + ([] if first else [acc, rows, rows]),
            out_specs=out_specs,
            scratch_shapes=scratch,
        ),
        out_shape=out_shape,
        compiler_params=pltpu.CompilerParams(vmem_limit_bytes=32 * 2**20),
        cost_estimate=pl.CostEstimate(
            flops=block, bytes_accessed=block, transcendentals=0
        ),
        name="attend_forward",
    )(q, kv, kv, ids_q, ids_k, *([] if first else state))


def backward_kernel(
    first, last, pairs, q_ref, g_ref, k_ref, v_ref, o_ref, total_ref, ids_q_ref, ids_k_ref, *refs
):
    if not first:
        grad_q_in, refs = refs[0], refs[1:]
    grad_kv, sums, grad_q_out, grad_q, kind_ref, bias_ref = refs if last else refs[:2] + (None,) + refs[2:]
    if first:
        grad_q[...] = jnp.zeros_like(grad_q)
    else:
        grad_q[...] = grad_q_in[...]
    look(kind_ref, bias_ref, ids_q_ref, ids_k_ref)
    step = pl.program_id(0)
    k_columns = pl.ds(pl.multiple_of(step * PAIR, PAIR), PAIR)
    v_columns = pl.ds(pl.multiple_of((step + pairs) * PAIR, PAIR), PAIR)

    def visit(masked):
        q, g, k, v = q_ref[...], g_ref[...], k_ref[...], v_ref[...]
        k_t = k.T
        products = high(g).T * o_ref[...]
        sum_k = sum_v = None
        for half in range(2):
            rows = head_rows(half)
            q_half, g_half = lane_half(q, half), lane_half(g, half)
            delta = jnp.sum(products[rows], axis=0, keepdims=True)
            scores = dot(k, q_half, NT)
            if masked:
                scores = scores + bias_ref[...]
            prob = jnp.exp(scores - total_ref[0, half : half + 1, :])
            grad_prob = dot(v, g_half, NT)
            grad_score = low(prob * (grad_prob - delta))
            part_v = dot(low(prob), g_half, NN)
            part_k = dot(grad_score, q_half, NN)
            sum_v = part_v if sum_v is None else sum_v + part_v
            sum_k = part_k if sum_k is None else sum_k + part_k
            grad_q[rows, :] += dot(k_t[rows], grad_score, NN)
        grad_kv[:, k_columns] = low(sum_k)
        grad_kv[:, v_columns] = low(sum_v)
        sums[0:1, k_columns] = jnp.sum(high(low(sum_v)), axis=0, keepdims=True)

    pl.when(kind_ref[0] == 1)(functools.partial(visit, False))
    pl.when(kind_ref[0] == 2)(functools.partial(visit, True))

    @pl.when(kind_ref[0] == 0)
    def _():
        nothing = jnp.zeros((grad_kv.shape[0], PAIR), jnp.bfloat16)
        grad_kv[:, k_columns] = nothing
        grad_kv[:, v_columns] = nothing
        sums[0:1, k_columns] = jnp.zeros((1, PAIR), jnp.float32)

    if last:
        grad_queries = low(grad_q[...].T * HEAD_DIM ** (-0.5))
        grad_q_out[...] = grad_queries
        sums[1:2, k_columns] = jnp.sum(high(grad_queries), axis=0, keepdims=True)


def attend_backward(phase, q, g, kv, attended_t, totals, ids_q, ids_k, grad_q, last):
    block, width = q.shape
    all_pairs = width // PAIR
    pairs = all_pairs // PHASES
    offset = phase * pairs
    first = grad_q is None
    mine = pl.BlockSpec((block, PAIR), lambda p: (0, p + offset))
    acc = pl.BlockSpec((PAIR, block), lambda p: (p, 0))
    out_specs = [
        pl.BlockSpec((block, 2 * pairs * PAIR), lambda p: (0, 0)),
        pl.BlockSpec((2, pairs * PAIR), lambda p: (0, 0)),
    ]
    out_shape = [
        jax.ShapeDtypeStruct((block, 2 * pairs * PAIR), jnp.bfloat16),
        jax.ShapeDtypeStruct((2, pairs * PAIR), jnp.float32),
    ]
    scratch = [pltpu.SMEM((1,), jnp.int32), pltpu.VMEM((block, block), jnp.float32)]
    if last:
        out_specs += [pl.BlockSpec((block, PAIR), lambda p: (0, p))]
        out_shape += [jax.ShapeDtypeStruct((block, pairs * PAIR), jnp.bfloat16)]
        scratch = [pltpu.VMEM((PAIR, block), jnp.float32)] + scratch
    else:
        out_specs += [acc]
        out_shape += [jax.ShapeDtypeStruct((pairs * PAIR, block), jnp.float32)]
    return pl.pallas_call(
        functools.partial(backward_kernel, first, last, pairs),
        grid_spec=pl.GridSpec(
            grid=(pairs,),
            in_specs=[
                mine,
                mine,
                mine,
                pl.BlockSpec((block, PAIR), lambda p: (0, p + offset + all_pairs)),
                pl.BlockSpec((PAIR, block), lambda p: (p + offset, 0)),
                pl.BlockSpec((1, 2, block), lambda p: (p + offset, 0, 0)),
                pl.BlockSpec((1, block), lambda p: (0, 0)),
                pl.BlockSpec((block, 1), lambda p: (0, 0)),
            ]
            + ([] if first else [acc]),
            out_specs=out_specs,
            scratch_shapes=scratch,
        ),
        out_shape=out_shape,
        compiler_params=pltpu.CompilerParams(vmem_limit_bytes=32 * 2**20),
        cost_estimate=pl.CostEstimate(
            flops=block, bytes_accessed=block, transcendentals=0
        ),
        name="attend_backward",
    )(q, g, kv, kv, attended_t, totals, ids_q, ids_k, *([] if first else [grad_q]))


def layer_norm(values, gain, shift):
    center = values - jnp.mean(values, axis=-1, keepdims=True)
    inverse = lax.rsqrt(jnp.mean(center * center, axis=-1, keepdims=True) + EPSILON)
    scaled = center * inverse
    return scaled * gain + shift, scaled, inverse


def norm_back(grad_out, scaled, inverse, gain):
    grad_scaled = grad_out * gain
    grad_in = inverse * (
        grad_scaled
        - jnp.mean(grad_scaled, axis=-1, keepdims=True)
        - scaled * jnp.mean(grad_scaled * scaled, axis=-1, keepdims=True)
    )
    return grad_in, jnp.sum(grad_out * scaled, axis=0), jnp.sum(grad_out, axis=0)


def pick(x, index, parts):
    size = x.shape[0] // parts
    return lax.dynamic_slice_in_dim(x, index * size, size, 0)


def add_low(left, right):
    return low(high(left) + high(right))


def steps_of(batch, seq):
    chips = [1 << i for i in range(1, batch.bit_length() - 1)]
    places = [1 << i for i in range(seq.bit_length() - 1)]
    return [("batch", 1, 1), *(("batch", a, b) for a, b in zip(chips, chips[::-1])), *(("seq", p, p) for p in places)]


def partner(x, step, counts):
    axis, even, odd = step
    if axis == "seq":
        paths = [(i, i ^ even) for i in range(counts["seq"])]
    else:
        paths = [(i, i ^ (odd if i % 2 else even)) for i in range(counts["batch"])]
    return x, lambda x: lax.ppermute(x, axis, paths)


def side_of(step):
    axis, even, odd = step
    index = lax.axis_index(axis)
    if even == odd:
        return (index // even) % 2
    return jnp.where(lax.axis_index("batch") % 2 == 0, (index // even) % 2, (index // odd) % 2)


def join(x, other, side):
    return jnp.where(side == 0, jnp.concatenate([x, other], axis=0), jnp.concatenate([other, x], axis=0))


def passed(x, step, counts):
    x, call = partner(x, step, counts)
    return call(x)


def down(x, step, counts):
    side = side_of(step)
    return add_low(pick(x, side, 2), passed(pick(x, 1 - side, 2), step, counts))


def up(x, step, counts):
    return join(x, passed(x, step, counts), side_of(step))


def up_last(x, step, counts, cuts):
    got = passed(x, step, counts)
    edges = [0, *cuts, x.shape[1]]
    return [high(join(x[:, a:b], got[:, a:b], side_of(step))) for a, b in zip(edges[:-1], edges[1:])]


def apart(certain, run):
    shapes = jax.eval_shape(run)
    return lax.cond(certain, run, lambda: jax.tree.map(lambda x: jnp.zeros(x.shape, x.dtype), shapes))


def visits(me, seq):
    short, long = (("L", me), ("R", seq - 1 - me))
    if short[1] > long[1]:
        short, long = long, short
    order = []
    for k in range(1, short[1] + 1):
        order += [(short[0], k), (long[0], k)]
    return order + [(long[0], k) for k in range(short[1] + 1, long[1] + 1)]


def choose(me, options):
    known = [(i, x) for i, x in enumerate(options) if x is not None]
    value = known[-1][1]
    for i, x in reversed(known[:-1]):
        if x is not value:
            value = jnp.where(me == i, x, value)
    return value


def pack_ids(ids, width):
    whole = jnp.zeros((8, width), jnp.bfloat16)
    both = jnp.stack([ids // ID_BASE, ids % ID_BASE]).astype(jnp.bfloat16)
    return lax.dynamic_update_slice(whole, both, (0, 0))


def unpack_ids(rows, block):
    rows = rows[:, :block].astype(jnp.int32)
    return rows[0] * ID_BASE + rows[1]


def shards(
    batch,
    seq,
    hidden_in,
    document_ids,
    query_weight,
    query_bias,
    key_weight,
    value_weight,
    value_bias,
    proj_weight,
    proj_bias,
    first_gain,
    first_shift,
    inner_weight,
    inner_bias,
    outer_weight,
    outer_bias,
    second_gain,
    second_shift,
    output_grad,
):
    hidden = hidden_in[0]
    ids = document_ids[0]
    block, width = hidden.shape
    half = width // PHASES
    me = lax.axis_index("seq")
    counts = {"batch": batch, "seq": seq}

    orders = [visits(i, seq) for i in range(seq)]

    came = {("L", 0): jnp.concatenate([hidden, pack_ids(ids, width)], axis=0)}
    came["R", 0] = came["L", 0]

    kv_weight = jnp.concatenate([key_weight, value_weight], axis=1)
    kv_bias = jnp.concatenate([jnp.zeros_like(value_bias), value_bias])
    queries = low(times(hidden, query_weight) + query_bias) * jnp.bfloat16(HEAD_DIM ** (-0.5))
    ids_q = ids[None, :]
    state = None
    kept = []
    for s in range(seq):
        if s < seq - 1:
            to_right = lax.ppermute(came["L", s], "seq", [(i, i + 1) for i in range(s, seq - 1)])
            to_left = lax.ppermute(came["R", s], "seq", [(i, i - 1) for i in range(1, seq - s)])
        if s == 0:
            packed, ids_k = came["L", 0], ids
        else:
            packed = choose(me, [came[orders[i][s - 1]] for i in range(seq)])
            ids_k = unpack_ids(packed[block:], block)
        tokens = hidden if s == 0 else packed[:block]
        kv = low(times(tokens, kv_weight) + kv_bias)
        state = attend_forward(queries, kv, ids_q, ids_k[:, None], state, s == seq - 1)
        if s < seq - 1:
            came["L", s + 1], came["R", s + 1], state = lax.optimization_barrier((to_right, to_left, state))
        kept.append((hidden if s == 0 else packed, kv, ids_k[:, None]))
    attended_t, totals, attended = state

    branch = times(attended, proj_weight) + proj_bias
    first, first_scaled, first_inverse = layer_norm(high(hidden) + branch, first_gain, first_shift)
    first_low = low(first)
    inner_act = times(first_low, inner_weight) + inner_bias
    chance = 0.5 * (1.0 + lax.erf(inner_act * ROOT_HALF))
    activated = low(inner_act * chance)
    slope = low(chance + inner_act * (ROOT_TAU * jnp.exp(-0.5 * inner_act * inner_act)))
    activated, slope = lax.optimization_barrier((activated, slope))
    outer_act = times(activated, outer_weight) + outer_bias
    second, second_scaled, second_inverse = layer_norm(first + outer_act, second_gain, second_shift)
    result = low(second)
    grad_mix, grad_second_gain, grad_second_shift = norm_back(
        high(output_grad[0]), second_scaled, second_inverse, second_gain
    )
    grad_outer = low(grad_mix)
    grad_outer_bias = column_sums(grad_outer)
    grad_inner = low(times_back(grad_outer, outer_weight) * high(slope))
    early = (low(weight_grad(activated, grad_outer)), low(weight_grad(first_low, grad_inner)))
    early, grad_inner = lax.optimization_barrier((early, grad_inner))
    early_sums = lax.psum(early, ("batch", "seq"))

    certain = ids[0] >= 0
    steps = steps_of(**counts)
    far = len(steps) - 1

    def attention_part():
        grad_inner_bias = column_sums(grad_inner)
        grad_first = grad_mix + times_back(grad_inner, inner_weight)
        grad_resid, grad_first_gain, grad_first_shift = norm_back(
            grad_first, first_scaled, first_inverse, first_gain
        )
        grad_branch = low(grad_resid)
        grad_attended = low(times_back(grad_branch, proj_weight))
        grad_query = None
        kv_grad = 0.0
        grad_value_bias = 0.0
        terms = {}
        for s in reversed(range(seq)):
            packed, kv, ids_k = kept[s]
            grad_kv, sums, grad_query = attend_backward(
                0, queries, grad_attended, kv, attended_t, totals, ids_q, ids_k, grad_query, s == 0
            )
            kv_grad += weight_grad(packed[:block], grad_kv)
            grad_value_bias += sums[0]
            terms[s] = low(times_back(grad_kv, kv_weight))
        late = jnp.concatenate(
            [low(weight_grad(hidden, grad_query)), low(kv_grad), low(weight_grad(attended, grad_branch))], axis=1
        )
        vectors = jnp.stack(
            [
                sums[1],
                grad_value_bias,
                column_sums(grad_branch),
                grad_first_gain,
                grad_first_shift,
                grad_outer_bias,
                grad_second_gain,
                grad_second_shift,
                *jnp.split(grad_inner_bias, inner_weight.shape[1] // width),
            ]
        )
        own_terms = grad_resid + high(terms[0]) + times_back(grad_query, query_weight)
        vectors = vectors + passed(vectors, steps[0], counts)
        return down(late, steps[0], counts), vectors, own_terms, [terms[s] for s in range(1, seq)]

    late, sums, own_terms, terms = apart(certain, attention_part)
    terms = dict(enumerate(terms, 1))

    def homeward(s):
        found = []
        for side in "LR":
            options = [terms[orders[i].index((side, s)) + 1] if (side, s) in orders[i] else None for i in range(seq)]
            found.append(choose(me, options))
        return found

    def send(s, sends):
        return [
            lax.ppermute(sends[0], "seq", [(i, i - 1) for i in range(s, seq)]),
            lax.ppermute(sends[1], "seq", [(i, i + 1) for i in range(seq - s)]),
        ]

    chips = [i for i, step in enumerate(steps) if i > 0 and step[0] == "batch"]
    places = [i for i, step in enumerate(steps) if step[0] == "seq"]

    def down_chips(late, sums):
        for i in chips:
            sums = sums + passed(sums, steps[i], counts)
            late = down(late, steps[i], counts)
        return late, sums, {s: homeward(s) for s in range(1, seq - 1)}

    def along_row(late, sums):
        for i in places:
            sums = sums + passed(sums, steps[i], counts)
            late = down(late, steps[i], counts)
        for i in places[::-1]:
            late = up(late, steps[i], counts)
        return late, sums

    late, on_way = lax.optimization_barrier((late, homeward(seq - 1)))
    on_way = send(seq - 1, on_way)
    late, sums, found = apart(certain, functools.partial(down_chips, late, sums))
    on_way, late, sums = lax.optimization_barrier((on_way, late, sums))
    late, sums = apart(certain, functools.partial(along_row, late, sums))
    work = [functools.partial(lambda i, x: up(x, steps[i], counts), i) for i in chips[::-1]]
    for s in reversed(range(1, seq - 1)):
        totals_home = [low(high(x) + high(o)) for x, o in zip(found[s], on_way)]
        late, totals_home = lax.optimization_barrier((late, totals_home))
        on_way = send(s, totals_home)
        if s == seq - 2:
            for i, run in enumerate(work):
                if i == len(work) - 1:
                    late, early_sums = apart(
                        certain, lambda x=late: (run(x), [high(y) for y in early_sums])
                    )
                else:
                    late = apart(certain, functools.partial(run, late))
                late, early_sums = lax.optimization_barrier((late, early_sums))
            on_way, late = lax.optimization_barrier((on_way, late))
    late = apart(
        certain, lambda: up_last(late, steps[0], counts, (width, 2 * width, 3 * width))
    )
    vectors = sums
    grad_query_weight, grad_key_weight, grad_value_weight, grad_proj_weight = late
    grad_input = low(own_terms + high(on_way[0]) + high(on_way[1]))
    grad_outer_weight, grad_inner_weight = early_sums
    (
        grad_query_bias,
        grad_value_bias,
        grad_proj_bias,
        grad_first_gain,
        grad_first_shift,
        grad_outer_bias,
        grad_second_gain,
        grad_second_shift,
    ) = (vectors[i] for i in range(8))
    grad_inner_bias = vectors[8:].reshape(-1)
    return (
        result[None],
        grad_input[None],
        grad_query_weight,
        grad_query_bias,
        grad_key_weight,
        grad_value_weight,
        grad_value_bias,
        grad_proj_weight,
        grad_proj_bias,
        grad_first_gain,
        grad_first_shift,
        grad_inner_weight,
        grad_inner_bias,
        grad_outer_weight,
        grad_outer_bias,
        grad_second_gain,
        grad_second_shift,
    )


def solution(mesh):
    rows = P("batch", "seq", None)
    return jax.shard_map(
        functools.partial(shards, mesh.shape["batch"], mesh.shape["seq"]),
        mesh=mesh,
        in_specs=(rows, P("batch", "seq")) + (P(),) * 15 + (rows,),
        out_specs=(rows, rows) + (P(),) * 15,
        check_vma=False,
    )
```

```python
import functools

import jax
import jax.numpy as jnp
from jax import lax
from jax.experimental import pallas as pl
from jax.experimental.pallas import tpu as pltpu
from jax.sharding import PartitionSpec as P

HEAD_DIM = 64
PAIR = 2 * HEAD_DIM
MASKED = -1e30
EPSILON = 1e-05
ROOT_HALF = 0.7071067811865476
ROOT_TAU = 0.3989422804014327
PHASES = 1
ID_BASE = 128

NT = (((1,), (1,)), ((), ()))
NN = (((1,), (0,)), ((), ()))
TN = (((0,), (0,)), ((), ()))


def dot(left, right, dims):
    return lax.dot_general(left, right, dims, preferred_element_type=jnp.float32)


def low(x):
    return x.astype(jnp.bfloat16)


def high(x):
    return x.astype(jnp.float32)


def times(left, right):
    return dot(left, right, NN)


def times_back(left, right):
    return dot(left, right, NT)


def weight_grad(left, right):
    return dot(left, right, TN)


def column_sums(x):
    return jnp.sum(high(x), axis=0)


def lane_half(x, half):
    lanes = lax.broadcasted_iota(jnp.int32, x.shape, 1)
    keep = lanes < HEAD_DIM if half == 0 else lanes >= HEAD_DIM
    return jnp.where(keep, x, jnp.zeros_like(x))


def head_rows(half):
    return slice(half * HEAD_DIM, (half + 1) * HEAD_DIM)


def look(kind_ref, bias_ref, ids_q_ref, ids_k_ref):
    @pl.when(pl.program_id(0) == 0)
    def _():
        ids_q, ids_k = ids_q_ref[...], ids_k_ref[...]
        low_q, high_q, low_k, high_k = jnp.min(ids_q), jnp.max(ids_q), jnp.min(ids_k), jnp.max(ids_k)
        apart = (high_q < low_k) | (high_k < low_q)
        one = (low_q == high_k) & (low_k == high_q)
        kind_ref[0] = jnp.where(apart, 0, jnp.where(one, 1, 2)).astype(jnp.int32)

        @pl.when(kind_ref[0] == 2)
        def _():
            bias_ref[...] = jnp.where(ids_k == ids_q, 0.0, MASKED)


def forward_kernel(first, last, q_ref, k_ref, v_ref, ids_q_ref, ids_k_ref, *refs):
    if first:
        acc_in = peak_in = sum_in = None
    else:
        acc_in, peak_in, sum_in = refs[:3]
        refs = refs[3:]
    if last:
        acc_out, total_out, attended_out, acc, peak, sums, kind_ref, bias_ref = refs
    else:
        acc, peak, sums, kind_ref, bias_ref = refs
    if first:
        acc[...] = jnp.zeros_like(acc)
        sums[...] = jnp.zeros_like(sums)
        peak[...] = jnp.full(peak.shape, MASKED, jnp.float32)
    else:
        acc[...] = acc_in[...]
        sums[...] = sum_in[...]
        peak[...] = peak_in[...]
    look(kind_ref, bias_ref, ids_q_ref, ids_k_ref)

    def visit(masked):
        q, k = q_ref[...], k_ref[...]
        v_t = v_ref[...].T
        ones = jnp.ones((16, k.shape[0]), jnp.bfloat16)
        scores = [dot(k, lane_half(q, half), NT) for half in range(2)]
        if masked:
            scores = [x + bias_ref[...] for x in scores]
        old = [peak[0, half : half + 1, :] for half in range(2)]
        new = [jnp.maximum(o, jnp.max(x, axis=0, keepdims=True)) for o, x in zip(old, scores)]
        prob = [low(jnp.exp(x - m)) for x, m in zip(scores, new)]
        for half in range(2):
            shrink = jnp.exp(old[half] - new[half])
            rows, one = head_rows(half), slice(half, half + 1)
            mixed = dot(jnp.concatenate([v_t[rows], ones], axis=0), prob[half], NN)
            acc[rows, :] = acc[rows, :] * shrink + mixed[:HEAD_DIM]
            sums[0, one, :] = sums[0, one, :] * shrink + mixed[HEAD_DIM : HEAD_DIM + 1]
            peak[0, one, :] = new[half]

    pl.when(kind_ref[0] == 1)(functools.partial(visit, False))
    pl.when(kind_ref[0] == 2)(functools.partial(visit, True))

    if last:
        for half in range(2):
            rows, one = head_rows(half), slice(half, half + 1)
            acc_out[rows, :] = acc[rows, :] / sums[0, one, :]
            total_out[0, one, :] = peak[0, one, :] + jnp.log(sums[0, one, :])
        attended_out[...] = low(acc_out[...].T)


def attend_forward(q, kv, ids_q, ids_k, state, last):
    block, width = q.shape
    pairs = width // PAIR
    first = state is None
    rows = pl.BlockSpec((1, 2, block), lambda p: (p, 0, 0))
    acc = pl.BlockSpec((PAIR, block), lambda p: (p, 0))
    mine = pl.BlockSpec((block, PAIR), lambda p: (0, p))
    acc_shape = jax.ShapeDtypeStruct((width, block), jnp.float32)
    row_shape = jax.ShapeDtypeStruct((pairs, 2, block), jnp.float32)
    scratch = [pltpu.SMEM((1,), jnp.int32), pltpu.VMEM((block, block), jnp.float32)]
    if last:
        out_specs = [acc, rows, mine]
        out_shape = [acc_shape, row_shape, jax.ShapeDtypeStruct((block, width), jnp.bfloat16)]
        scratch = [
            pltpu.VMEM((PAIR, block), jnp.float32),
            pltpu.VMEM((1, 2, block), jnp.float32),
            pltpu.VMEM((1, 2, block), jnp.float32),
        ] + scratch
    else:
        out_specs, out_shape = [acc, rows, rows], [acc_shape, row_shape, row_shape]
    return pl.pallas_call(
        functools.partial(forward_kernel, first, last),
        grid_spec=pl.GridSpec(
            grid=(pairs,),
            in_specs=[
                mine,
                mine,
                pl.BlockSpec((block, PAIR), lambda p: (0, p + pairs)),
                pl.BlockSpec((1, block), lambda p: (0, 0)),
                pl.BlockSpec((block, 1), lambda p: (0, 0)),
            ]
            + ([] if first else [acc, rows, rows]),
            out_specs=out_specs,
            scratch_shapes=scratch,
        ),
        out_shape=out_shape,
        compiler_params=pltpu.CompilerParams(vmem_limit_bytes=32 * 2**20),
        cost_estimate=pl.CostEstimate(
            flops=block, bytes_accessed=block, transcendentals=0
        ),
        name="attend_forward",
    )(q, kv, kv, ids_q, ids_k, *([] if first else state))


def backward_kernel(
    first, last, pairs, q_ref, g_ref, k_ref, v_ref, o_ref, total_ref, ids_q_ref, ids_k_ref, *refs
):
    if not first:
        grad_q_in, refs = refs[0], refs[1:]
    grad_kv, sums, grad_q_out, grad_q, kind_ref, bias_ref = refs if last else refs[:2] + (None,) + refs[2:]
    if first:
        grad_q[...] = jnp.zeros_like(grad_q)
    else:
        grad_q[...] = grad_q_in[...]
    look(kind_ref, bias_ref, ids_q_ref, ids_k_ref)
    step = pl.program_id(0)
    k_columns = pl.ds(pl.multiple_of(step * PAIR, PAIR), PAIR)
    v_columns = pl.ds(pl.multiple_of((step + pairs) * PAIR, PAIR), PAIR)

    def visit(masked):
        q, g, k, v = q_ref[...], g_ref[...], k_ref[...], v_ref[...]
        k_t = k.T
        products = high(g).T * o_ref[...]
        sum_k = sum_v = None
        for half in range(2):
            rows = head_rows(half)
            q_half, g_half = lane_half(q, half), lane_half(g, half)
            delta = jnp.sum(products[rows], axis=0, keepdims=True)
            scores = dot(k, q_half, NT)
            if masked:
                scores = scores + bias_ref[...]
            prob = jnp.exp(scores - total_ref[0, half : half + 1, :])
            grad_prob = dot(v, g_half, NT)
            grad_score = low(prob * (grad_prob - delta))
            part_v = dot(low(prob), g_half, NN)
            part_k = dot(grad_score, q_half, NN)
            sum_v = part_v if sum_v is None else sum_v + part_v
            sum_k = part_k if sum_k is None else sum_k + part_k
            grad_q[rows, :] += dot(k_t[rows], grad_score, NN)
        grad_kv[:, k_columns] = low(sum_k)
        grad_kv[:, v_columns] = low(sum_v)
        sums[0:1, k_columns] = jnp.sum(high(low(sum_v)), axis=0, keepdims=True)

    pl.when(kind_ref[0] == 1)(functools.partial(visit, False))
    pl.when(kind_ref[0] == 2)(functools.partial(visit, True))

    @pl.when(kind_ref[0] == 0)
    def _():
        nothing = jnp.zeros((grad_kv.shape[0], PAIR), jnp.bfloat16)
        grad_kv[:, k_columns] = nothing
        grad_kv[:, v_columns] = nothing
        sums[0:1, k_columns] = jnp.zeros((1, PAIR), jnp.float32)

    if last:
        grad_queries = low(grad_q[...].T * HEAD_DIM ** (-0.5))
        grad_q_out[...] = grad_queries
        sums[1:2, k_columns] = jnp.sum(high(grad_queries), axis=0, keepdims=True)


def attend_backward(phase, q, g, kv, attended_t, totals, ids_q, ids_k, grad_q, last):
    block, width = q.shape
    all_pairs = width // PAIR
    pairs = all_pairs // PHASES
    offset = phase * pairs
    first = grad_q is None
    mine = pl.BlockSpec((block, PAIR), lambda p: (0, p + offset))
    acc = pl.BlockSpec((PAIR, block), lambda p: (p, 0))
    out_specs = [
        pl.BlockSpec((block, 2 * pairs * PAIR), lambda p: (0, 0)),
        pl.BlockSpec((2, pairs * PAIR), lambda p: (0, 0)),
    ]
    out_shape = [
        jax.ShapeDtypeStruct((block, 2 * pairs * PAIR), jnp.bfloat16),
        jax.ShapeDtypeStruct((2, pairs * PAIR), jnp.float32),
    ]
    scratch = [pltpu.SMEM((1,), jnp.int32), pltpu.VMEM((block, block), jnp.float32)]
    if last:
        out_specs += [pl.BlockSpec((block, PAIR), lambda p: (0, p))]
        out_shape += [jax.ShapeDtypeStruct((block, pairs * PAIR), jnp.bfloat16)]
        scratch = [pltpu.VMEM((PAIR, block), jnp.float32)] + scratch
    else:
        out_specs += [acc]
        out_shape += [jax.ShapeDtypeStruct((pairs * PAIR, block), jnp.float32)]
    return pl.pallas_call(
        functools.partial(backward_kernel, first, last, pairs),
        grid_spec=pl.GridSpec(
            grid=(pairs,),
            in_specs=[
                mine,
                mine,
                mine,
                pl.BlockSpec((block, PAIR), lambda p: (0, p + offset + all_pairs)),
                pl.BlockSpec((PAIR, block), lambda p: (p + offset, 0)),
                pl.BlockSpec((1, 2, block), lambda p: (p + offset, 0, 0)),
                pl.BlockSpec((1, block), lambda p: (0, 0)),
                pl.BlockSpec((block, 1), lambda p: (0, 0)),
            ]
            + ([] if first else [acc]),
            out_specs=out_specs,
            scratch_shapes=scratch,
        ),
        out_shape=out_shape,
        compiler_params=pltpu.CompilerParams(vmem_limit_bytes=32 * 2**20),
        cost_estimate=pl.CostEstimate(
            flops=block, bytes_accessed=block, transcendentals=0
        ),
        name="attend_backward",
    )(q, g, kv, kv, attended_t, totals, ids_q, ids_k, *([] if first else [grad_q]))


def layer_norm(values, gain, shift):
    center = values - jnp.mean(values, axis=-1, keepdims=True)
    inverse = lax.rsqrt(jnp.mean(center * center, axis=-1, keepdims=True) + EPSILON)
    scaled = center * inverse
    return scaled * gain + shift, scaled, inverse


def norm_back(grad_out, scaled, inverse, gain):
    grad_scaled = grad_out * gain
    grad_in = inverse * (
        grad_scaled
        - jnp.mean(grad_scaled, axis=-1, keepdims=True)
        - scaled * jnp.mean(grad_scaled * scaled, axis=-1, keepdims=True)
    )
    return grad_in, jnp.sum(grad_out * scaled, axis=0), jnp.sum(grad_out, axis=0)


def pick(x, index, parts):
    size = x.shape[0] // parts
    return lax.dynamic_slice_in_dim(x, index * size, size, 0)


def add_low(left, right):
    return low(high(left) + high(right))


def steps_of(batch, seq):
    chips = [1 << i for i in range(1, batch.bit_length() - 1)]
    places = [1 << i for i in range(seq.bit_length() - 1)]
    return [("batch", 1, 1), *(("batch", a, b) for a, b in zip(chips, chips[::-1])), *(("seq", p, p) for p in places)]


def partner(x, step, counts):
    axis, even, odd = step
    if axis == "seq":
        paths = [(i, i ^ even) for i in range(counts["seq"])]
    else:
        paths = [(i, i ^ (odd if i % 2 else even)) for i in range(counts["batch"])]
    return x, lambda x: lax.ppermute(x, axis, paths)


def side_of(step):
    axis, even, odd = step
    index = lax.axis_index(axis)
    if even == odd:
        return (index // even) % 2
    return jnp.where(lax.axis_index("batch") % 2 == 0, (index // even) % 2, (index // odd) % 2)


def join(x, other, side):
    return jnp.where(side == 0, jnp.concatenate([x, other], axis=0), jnp.concatenate([other, x], axis=0))


def passed(x, step, counts):
    x, call = partner(x, step, counts)
    return call(x)


def down(x, step, counts):
    side = side_of(step)
    return add_low(pick(x, side, 2), passed(pick(x, 1 - side, 2), step, counts))


def parted(x, step):
    side = side_of(step)
    return pick(x, side, 2), pick(x, 1 - side, 2)


def up(x, step, counts):
    return join(x, passed(x, step, counts), side_of(step))


def up_last(x, step, counts, cuts):
    got = passed(x, step, counts)
    edges = [0, *cuts, x.shape[1]]
    return [high(join(x[:, a:b], got[:, a:b], side_of(step))) for a, b in zip(edges[:-1], edges[1:])]


def apart(certain, run):
    shapes = jax.eval_shape(run)
    return lax.cond(certain, run, lambda: jax.tree.map(lambda x: jnp.zeros(x.shape, x.dtype), shapes))


def visits(me, seq):
    short, long = (("L", me), ("R", seq - 1 - me))
    if short[1] > long[1]:
        short, long = long, short
    order = []
    for k in range(1, short[1] + 1):
        order += [(short[0], k), (long[0], k)]
    return order + [(long[0], k) for k in range(short[1] + 1, long[1] + 1)]


def choose(me, options):
    known = [(i, x) for i, x in enumerate(options) if x is not None]
    value = known[-1][1]
    for i, x in reversed(known[:-1]):
        if x is not value:
            value = jnp.where(me == i, x, value)
    return value


def pack_ids(ids, width):
    whole = jnp.zeros((8, width), jnp.bfloat16)
    both = jnp.stack([ids // ID_BASE, ids % ID_BASE]).astype(jnp.bfloat16)
    return lax.dynamic_update_slice(whole, both, (0, 0))


def unpack_ids(rows, block):
    rows = rows[:, :block].astype(jnp.int32)
    return rows[0] * ID_BASE + rows[1]


def shards(
    batch,
    seq,
    hidden_in,
    document_ids,
    query_weight,
    query_bias,
    key_weight,
    value_weight,
    value_bias,
    proj_weight,
    proj_bias,
    first_gain,
    first_shift,
    inner_weight,
    inner_bias,
    outer_weight,
    outer_bias,
    second_gain,
    second_shift,
    output_grad,
):
    hidden = hidden_in[0]
    ids = document_ids[0]
    block, width = hidden.shape
    half = width // PHASES
    me = lax.axis_index("seq")
    counts = {"batch": batch, "seq": seq}

    orders = [visits(i, seq) for i in range(seq)]

    came = {("L", 0): jnp.concatenate([hidden, pack_ids(ids, width)], axis=0)}
    came["R", 0] = came["L", 0]

    kv_weight = jnp.concatenate([key_weight, value_weight], axis=1)
    kv_bias = jnp.concatenate([jnp.zeros_like(value_bias), value_bias])
    queries = low(times(hidden, query_weight) + query_bias) * jnp.bfloat16(HEAD_DIM ** (-0.5))
    ids_q = ids[None, :]
    state = None
    kept = []
    for s in range(seq):
        if s < seq - 1:
            to_right = lax.ppermute(came["L", s], "seq", [(i, i + 1) for i in range(s, seq - 1)])
            to_left = lax.ppermute(came["R", s], "seq", [(i, i - 1) for i in range(1, seq - s)])
        if s == 0:
            packed, ids_k = came["L", 0], ids
        else:
            packed = choose(me, [came[orders[i][s - 1]] for i in range(seq)])
            ids_k = unpack_ids(packed[block:], block)
        tokens = hidden if s == 0 else packed[:block]
        kv = low(times(tokens, kv_weight) + kv_bias)
        state = attend_forward(queries, kv, ids_q, ids_k[:, None], state, s == seq - 1)
        if s < seq - 1:
            came["L", s + 1], came["R", s + 1], state = lax.optimization_barrier((to_right, to_left, state))
        kept.append((hidden if s == 0 else packed, kv, ids_k[:, None]))
    attended_t, totals, attended = state

    branch = times(attended, proj_weight) + proj_bias
    first, first_scaled, first_inverse = layer_norm(high(hidden) + branch, first_gain, first_shift)
    first_low = low(first)
    inner_act = times(first_low, inner_weight) + inner_bias
    chance = 0.5 * (1.0 + lax.erf(inner_act * ROOT_HALF))
    activated = low(inner_act * chance)
    slope = low(chance + inner_act * (ROOT_TAU * jnp.exp(-0.5 * inner_act * inner_act)))
    activated, slope = lax.optimization_barrier((activated, slope))
    outer_act = times(activated, outer_weight) + outer_bias
    second, second_scaled, second_inverse = layer_norm(first + outer_act, second_gain, second_shift)
    result = low(second)
    grad_mix, grad_second_gain, grad_second_shift = norm_back(
        high(output_grad[0]), second_scaled, second_inverse, second_gain
    )
    grad_outer = low(grad_mix)
    grad_outer_bias = column_sums(grad_outer)
    grad_inner = low(times_back(grad_outer, outer_weight) * high(slope))
    early = (low(weight_grad(activated, grad_outer)), low(weight_grad(first_low, grad_inner)))
    early, grad_inner = lax.optimization_barrier((early, grad_inner))
    early_sums = lax.psum(early, ("batch", "seq"))

    certain = ids[0] >= 0
    steps = steps_of(**counts)
    far = len(steps) - 1

    chips = [i for i, step in enumerate(steps) if i > 0 and step[0] == "batch"]
    places = [i for i, step in enumerate(steps) if step[0] == "seq"]

    def attention_part():
        grad_first = grad_mix + times_back(grad_inner, inner_weight)
        grad_resid, grad_first_gain, grad_first_shift = norm_back(
            grad_first, first_scaled, first_inverse, first_gain
        )
        grad_branch = low(grad_resid)
        grad_attended = low(times_back(grad_branch, proj_weight))
        grad_query = None
        kv_grad = 0.0
        grad_value_bias = 0.0
        terms = {}
        for s in reversed(range(seq)):
            packed, kv, ids_k = kept[s]
            grad_kv, sums, grad_query = attend_backward(
                0, queries, grad_attended, kv, attended_t, totals, ids_q, ids_k, grad_query, s == 0
            )
            kv_grad += weight_grad(packed[:block], grad_kv)
            grad_value_bias += sums[0]
            terms[s] = low(times_back(grad_kv, kv_weight))
        late = jnp.concatenate(
            [low(weight_grad(hidden, grad_query)), low(kv_grad), low(weight_grad(attended, grad_branch))], axis=1
        )
        vectors = [sums[1], grad_value_bias, column_sums(grad_branch), grad_first_gain, grad_first_shift]
        own_terms = grad_resid + high(terms[0]) + times_back(grad_query, query_weight)
        return parted(down(late, steps[0], counts), steps[chips[0]]), vectors, own_terms, [terms[s] for s in range(1, seq)]

    late, sums, own_terms, terms = apart(certain, attention_part)
    terms = dict(enumerate(terms, 1))

    def homeward(s):
        found = []
        for side in "LR":
            options = [terms[orders[i].index((side, s)) + 1] if (side, s) in orders[i] else None for i in range(seq)]
            found.append(choose(me, options))
        return found

    def send(s, sends):
        return [
            lax.ppermute(sends[0], "seq", [(i, i - 1) for i in range(s, seq)]),
            lax.ppermute(sends[1], "seq", [(i, i + 1) for i in range(seq - s)]),
        ]


    def down_chips(late, vectors):
        sums = jnp.stack(
            [
                *vectors,
                grad_outer_bias,
                grad_second_gain,
                grad_second_shift,
                *jnp.split(column_sums(grad_inner), inner_weight.shape[1] // width),
            ]
        )
        sums = sums + passed(sums, steps[0], counts)
        for i in chips:
            sums = sums + passed(sums, steps[i], counts)
            if i == chips[0]:
                late = add_low(late[0], passed(late[1], steps[i], counts))
            else:
                late = down(late, steps[i], counts)
        return late, sums, {s: homeward(s) for s in range(1, seq - 1)}

    def along_row(late, sums, on_way):
        for i in places:
            sums = sums + passed(sums, steps[i], counts)
            late = down(late, steps[i], counts)
        for i in places[::-1]:
            late = up(late, steps[i], counts)
        return late, sums, [low(high(x) + high(o)) for x, o in zip(found[seq - 2], on_way)]

    late, on_way = lax.optimization_barrier((late, homeward(seq - 1)))
    on_way = send(seq - 1, on_way)
    late, sums, found = apart(certain, functools.partial(down_chips, late, sums))
    on_way, late, sums = lax.optimization_barrier((on_way, late, sums))
    late, sums, second = apart(certain, functools.partial(along_row, late, sums, on_way))
    def up_chips(late):
        for i in chips[::-1]:
            late = up(late, steps[i], counts)
        return late

    def last_part(late, early_sums):
        return up_last(late, steps[0], counts, (width, 2 * width, 3 * width)), [high(x) for x in early_sums]

    for s in reversed(range(1, seq - 1)):
        totals_home = second if s == seq - 2 else [low(high(x) + high(o)) for x, o in zip(found[s], on_way)]
        late, totals_home = lax.optimization_barrier((late, totals_home))
        on_way = send(s, totals_home)
        if s == seq - 2:
            late = apart(certain, functools.partial(up_chips, late))
            on_way, late = lax.optimization_barrier((on_way, late))
    late, early_sums = lax.optimization_barrier((late, early_sums))
    late, early_sums = apart(certain, functools.partial(last_part, late, early_sums))
    on_way, late, early_sums = lax.optimization_barrier((on_way, late, early_sums))
    vectors = sums
    grad_query_weight, grad_key_weight, grad_value_weight, grad_proj_weight = late
    grad_input = low(own_terms + high(on_way[0]) + high(on_way[1]))
    grad_outer_weight, grad_inner_weight = early_sums
    (
        grad_query_bias,
        grad_value_bias,
        grad_proj_bias,
        grad_first_gain,
        grad_first_shift,
        grad_outer_bias,
        grad_second_gain,
        grad_second_shift,
    ) = (vectors[i] for i in range(8))
    grad_inner_bias = vectors[8:].reshape(-1)
    return (
        result[None],
        grad_input[None],
        grad_query_weight,
        grad_query_bias,
        grad_key_weight,
        grad_value_weight,
        grad_value_bias,
        grad_proj_weight,
        grad_proj_bias,
        grad_first_gain,
        grad_first_shift,
        grad_inner_weight,
        grad_inner_bias,
        grad_outer_weight,
        grad_outer_bias,
        grad_second_gain,
        grad_second_shift,
    )


def solution(mesh):
    rows = P("batch", "seq", None)
    return jax.shard_map(
        functools.partial(shards, mesh.shape["batch"], mesh.shape["seq"]),
        mesh=mesh,
        in_specs=(rows, P("batch", "seq")) + (P(),) * 15 + (rows,),
        out_specs=(rows, rows) + (P(),) * 15,
        check_vma=False,
    )
```

```python
import functools

import jax
import jax.numpy as jnp
from jax import lax
from jax.experimental import pallas as pl
from jax.experimental.pallas import tpu as pltpu
from jax.sharding import PartitionSpec as P

HEAD_DIM = 64
PAIR = 2 * HEAD_DIM
MASKED = -1e30
GROUP = 2
EPSILON = 1e-05
ROOT_HALF = 0.7071067811865476
ROOT_TAU = 0.3989422804014327
ID_BASE = 128

NT = (((1,), (1,)), ((), ()))
NN = (((1,), (0,)), ((), ()))
TN = (((0,), (0,)), ((), ()))


def dot(left, right, dims):
    return lax.dot_general(left, right, dims, preferred_element_type=jnp.float32)


def low(x):
    return x.astype(jnp.bfloat16)


def high(x):
    return x.astype(jnp.float32)


def times(left, right):
    return dot(left, right, NN)


def times_back(left, right):
    return dot(left, right, NT)


def weight_grad(left, right):
    return dot(left, right, TN)


def column_sums(x):
    return jnp.sum(high(x), axis=0)


def lane_half(x, half):
    lanes = lax.broadcasted_iota(jnp.int32, x.shape, 1)
    keep = lanes < HEAD_DIM if half == 0 else lanes >= HEAD_DIM
    return jnp.where(keep, x, jnp.zeros_like(x))


def head_rows(half):
    return slice(half * HEAD_DIM, (half + 1) * HEAD_DIM)


def look(kind_ref, bias_ref, ids_q_ref, ids_k_ref):
    @pl.when(pl.program_id(0) == 0)
    def _():
        ids_q, ids_k = ids_q_ref[...], ids_k_ref[...]
        low_q, high_q, low_k, high_k = jnp.min(ids_q), jnp.max(ids_q), jnp.min(ids_k), jnp.max(ids_k)
        apart = (high_q < low_k) | (high_k < low_q)
        one = (low_q == high_k) & (low_k == high_q)
        kind_ref[0] = jnp.where(apart, 0, jnp.where(one, 1, 2)).astype(jnp.int32)

        @pl.when(kind_ref[0] == 2)
        def _():
            bias_ref[...] = jnp.where(ids_k == ids_q, 0.0, MASKED)


def forward_kernel(first, last, q_ref, k_ref, v_ref, ids_q_ref, ids_k_ref, *refs):
    if first:
        acc_in = peak_in = sum_in = None
    else:
        acc_in, peak_in, sum_in = refs[:3]
        refs = refs[3:]
    if last:
        acc_out, total_out, attended_out, acc, peak, sums, kind_ref, bias_ref = refs
    else:
        acc, peak, sums, kind_ref, bias_ref = refs
    if first:
        acc[...] = jnp.zeros_like(acc)
        sums[...] = jnp.zeros_like(sums)
        peak[...] = jnp.full(peak.shape, MASKED, jnp.float32)
    else:
        acc[...] = acc_in[...]
        sums[...] = sum_in[...]
        peak[...] = peak_in[...]
    look(kind_ref, bias_ref, ids_q_ref, ids_k_ref)

    def visit(masked):
        ones = jnp.ones((16, k_ref.shape[0]), jnp.bfloat16)
        for pair in range(GROUP):
            columns = slice(pair * PAIR, (pair + 1) * PAIR)
            q, k = q_ref[:, columns], k_ref[:, columns]
            v_t = v_ref[:, columns].T
            scores = [dot(k, lane_half(q, half), NT) for half in range(2)]
            if masked:
                scores = [x + bias_ref[...] for x in scores]
            old = [peak[pair, half : half + 1, :] for half in range(2)]
            new = [jnp.maximum(o, jnp.max(x, axis=0, keepdims=True)) for o, x in zip(old, scores)]
            prob = [low(jnp.exp(x - m)) for x, m in zip(scores, new)]
            for half in range(2):
                shrink = jnp.exp(old[half] - new[half])
                one = slice(half, half + 1)
                rows = slice(pair * PAIR + half * HEAD_DIM, pair * PAIR + (half + 1) * HEAD_DIM)
                mixed = dot(jnp.concatenate([v_t[head_rows(half)], ones], axis=0), prob[half], NN)
                acc[rows, :] = acc[rows, :] * shrink + mixed[:HEAD_DIM]
                sums[pair, one, :] = sums[pair, one, :] * shrink + mixed[HEAD_DIM : HEAD_DIM + 1]
                peak[pair, one, :] = new[half]

    pl.when(kind_ref[0] == 1)(functools.partial(visit, False))
    pl.when(kind_ref[0] == 2)(functools.partial(visit, True))

    if last:
        for pair in range(GROUP):
            for half in range(2):
                one = slice(half, half + 1)
                rows = slice(pair * PAIR + half * HEAD_DIM, pair * PAIR + (half + 1) * HEAD_DIM)
                acc_out[rows, :] = acc[rows, :] / sums[pair, one, :]
                total_out[pair, one, :] = peak[pair, one, :] + jnp.log(sums[pair, one, :])
            columns = slice(pair * PAIR, (pair + 1) * PAIR)
            attended_out[:, columns] = low(acc_out[columns, :].T)


def attend_forward(q, kv, ids_q, ids_k, state, last):
    block, width = q.shape
    pairs = width // PAIR
    first = state is None
    steps = pairs // GROUP
    rows = pl.BlockSpec((GROUP, 2, block), lambda p: (p, 0, 0))
    acc = pl.BlockSpec((GROUP * PAIR, block), lambda p: (p, 0))
    mine = pl.BlockSpec((block, GROUP * PAIR), lambda p: (0, p))
    acc_shape = jax.ShapeDtypeStruct((width, block), jnp.float32)
    row_shape = jax.ShapeDtypeStruct((pairs, 2, block), jnp.float32)
    scratch = [pltpu.SMEM((1,), jnp.int32), pltpu.VMEM((block, block), jnp.float32)]
    if last:
        out_specs = [acc, rows, mine]
        out_shape = [acc_shape, row_shape, jax.ShapeDtypeStruct((block, width), jnp.bfloat16)]
        scratch = [
            pltpu.VMEM((GROUP * PAIR, block), jnp.float32),
            pltpu.VMEM((GROUP, 2, block), jnp.float32),
            pltpu.VMEM((GROUP, 2, block), jnp.float32),
        ] + scratch
    else:
        out_specs, out_shape = [acc, rows, rows], [acc_shape, row_shape, row_shape]
    return pl.pallas_call(
        functools.partial(forward_kernel, first, last),
        grid_spec=pl.GridSpec(
            grid=(steps,),
            in_specs=[
                mine,
                mine,
                pl.BlockSpec((block, GROUP * PAIR), lambda p: (0, p + steps)),
                pl.BlockSpec((1, block), lambda p: (0, 0)),
                pl.BlockSpec((block, 1), lambda p: (0, 0)),
            ]
            + ([] if first else [acc, rows, rows]),
            out_specs=out_specs,
            scratch_shapes=scratch,
        ),
        out_shape=out_shape,
        compiler_params=pltpu.CompilerParams(vmem_limit_bytes=32 * 2**20),
        cost_estimate=pl.CostEstimate(
            flops=block, bytes_accessed=block, transcendentals=0
        ),
        name="attend_forward",
    )(q, kv, kv, ids_q, ids_k, *([] if first else state))


def backward_kernel(
    first, last, pairs, q_ref, g_ref, k_ref, v_ref, o_ref, total_ref, ids_q_ref, ids_k_ref, *refs
):
    if not first:
        grad_q_in, refs = refs[0], refs[1:]
    grad_kv, sums, grad_q_out, grad_q, kind_ref, bias_ref = refs if last else refs[:2] + (None,) + refs[2:]
    if first:
        grad_q[...] = jnp.zeros_like(grad_q)
    else:
        grad_q[...] = grad_q_in[...]
    look(kind_ref, bias_ref, ids_q_ref, ids_k_ref)
    step = pl.program_id(0)

    def columns_of(pair):
        at = step * GROUP + pair
        return pl.ds(pl.multiple_of(at * PAIR, PAIR), PAIR), pl.ds(pl.multiple_of((at + pairs) * PAIR, PAIR), PAIR)

    def visit(masked):
        for pair in range(GROUP):
            columns = slice(pair * PAIR, (pair + 1) * PAIR)
            k_columns, v_columns = columns_of(pair)
            q, g, k, v = q_ref[:, columns], g_ref[:, columns], k_ref[:, columns], v_ref[:, columns]
            k_t = k.T
            products = high(g).T * o_ref[columns, :]
            sum_k = sum_v = None
            for half in range(2):
                rows = head_rows(half)
                q_half, g_half = lane_half(q, half), lane_half(g, half)
                delta = jnp.sum(products[rows], axis=0, keepdims=True)
                scores = dot(k, q_half, NT)
                if masked:
                    scores = scores + bias_ref[...]
                prob = jnp.exp(scores - total_ref[pair, half : half + 1, :])
                grad_prob = dot(v, g_half, NT)
                grad_score = low(prob * (grad_prob - delta))
                part_v = dot(low(prob), g_half, NN)
                part_k = dot(grad_score, q_half, NN)
                sum_v = part_v if sum_v is None else sum_v + part_v
                sum_k = part_k if sum_k is None else sum_k + part_k
                mine = slice(pair * PAIR + half * HEAD_DIM, pair * PAIR + (half + 1) * HEAD_DIM)
                grad_q[mine, :] += dot(k_t[rows], grad_score, NN)
            grad_kv[:, k_columns] = low(sum_k)
            grad_kv[:, v_columns] = low(sum_v)
            sums[0:1, k_columns] = jnp.sum(high(low(sum_v)), axis=0, keepdims=True)

    pl.when(kind_ref[0] == 1)(functools.partial(visit, False))
    pl.when(kind_ref[0] == 2)(functools.partial(visit, True))

    @pl.when(kind_ref[0] == 0)
    def _():
        nothing = jnp.zeros((grad_kv.shape[0], PAIR), jnp.bfloat16)
        for pair in range(GROUP):
            k_columns, v_columns = columns_of(pair)
            grad_kv[:, k_columns] = nothing
            grad_kv[:, v_columns] = nothing
            sums[0:1, k_columns] = jnp.zeros((1, PAIR), jnp.float32)

    if last:
        for pair in range(GROUP):
            columns = slice(pair * PAIR, (pair + 1) * PAIR)
            grad_queries = low(grad_q[columns, :].T * HEAD_DIM ** (-0.5))
            grad_q_out[:, columns] = grad_queries
            sums[1:2, columns_of(pair)[0]] = jnp.sum(high(grad_queries), axis=0, keepdims=True)


def attend_backward(q, g, kv, attended_t, totals, ids_q, ids_k, grad_q, last):
    block, width = q.shape
    all_pairs = width // PAIR
    pairs = all_pairs
    steps = pairs // GROUP
    first = grad_q is None
    mine = pl.BlockSpec((block, GROUP * PAIR), lambda p: (0, p))
    acc = pl.BlockSpec((GROUP * PAIR, block), lambda p: (p, 0))
    out_specs = [
        pl.BlockSpec((block, 2 * pairs * PAIR), lambda p: (0, 0)),
        pl.BlockSpec((2, pairs * PAIR), lambda p: (0, 0)),
    ]
    out_shape = [
        jax.ShapeDtypeStruct((block, 2 * pairs * PAIR), jnp.bfloat16),
        jax.ShapeDtypeStruct((2, pairs * PAIR), jnp.float32),
    ]
    scratch = [pltpu.SMEM((1,), jnp.int32), pltpu.VMEM((block, block), jnp.float32)]
    if last:
        out_specs += [pl.BlockSpec((block, GROUP * PAIR), lambda p: (0, p))]
        out_shape += [jax.ShapeDtypeStruct((block, pairs * PAIR), jnp.bfloat16)]
        scratch = [pltpu.VMEM((GROUP * PAIR, block), jnp.float32)] + scratch
    else:
        out_specs += [acc]
        out_shape += [jax.ShapeDtypeStruct((pairs * PAIR, block), jnp.float32)]
    return pl.pallas_call(
        functools.partial(backward_kernel, first, last, pairs),
        grid_spec=pl.GridSpec(
            grid=(steps,),
            in_specs=[
                mine,
                mine,
                mine,
                pl.BlockSpec((block, GROUP * PAIR), lambda p: (0, p + steps)),
                pl.BlockSpec((GROUP * PAIR, block), lambda p: (p, 0)),
                pl.BlockSpec((GROUP, 2, block), lambda p: (p, 0, 0)),
                pl.BlockSpec((1, block), lambda p: (0, 0)),
                pl.BlockSpec((block, 1), lambda p: (0, 0)),
            ]
            + ([] if first else [acc]),
            out_specs=out_specs,
            scratch_shapes=scratch,
        ),
        out_shape=out_shape,
        compiler_params=pltpu.CompilerParams(vmem_limit_bytes=32 * 2**20),
        cost_estimate=pl.CostEstimate(
            flops=block, bytes_accessed=block, transcendentals=0
        ),
        name="attend_backward",
    )(q, g, kv, kv, attended_t, totals, ids_q, ids_k, *([] if first else [grad_q]))


def layer_norm(values, gain, shift):
    center = values - jnp.mean(values, axis=-1, keepdims=True)
    inverse = lax.rsqrt(jnp.mean(center * center, axis=-1, keepdims=True) + EPSILON)
    scaled = center * inverse
    return scaled * gain + shift, scaled, inverse


def norm_back(grad_out, scaled, inverse, gain):
    grad_scaled = grad_out * gain
    grad_in = inverse * (
        grad_scaled
        - jnp.mean(grad_scaled, axis=-1, keepdims=True)
        - scaled * jnp.mean(grad_scaled * scaled, axis=-1, keepdims=True)
    )
    return grad_in, jnp.sum(grad_out * scaled, axis=0), jnp.sum(grad_out, axis=0)


def pick(x, index, parts):
    size = x.shape[0] // parts
    return lax.dynamic_slice_in_dim(x, index * size, size, 0)


def add_low(left, right):
    return low(high(left) + high(right))


def steps_of(batch, seq):
    chips = [1 << i for i in range(1, batch.bit_length() - 1)]
    places = [1 << i for i in range(seq.bit_length() - 1)]
    return [("batch", 1, 1), *(("batch", a, b) for a, b in zip(chips, chips[::-1])), *(("seq", p, p) for p in places)]


def partner(x, step, counts):
    axis, even, odd = step
    if axis == "seq":
        paths = [(i, i ^ even) for i in range(counts["seq"])]
    else:
        paths = [(i, i ^ (odd if i % 2 else even)) for i in range(counts["batch"])]
    return x, lambda x: lax.ppermute(x, axis, paths)


def side_of(step):
    axis, even, odd = step
    index = lax.axis_index(axis)
    if even == odd:
        return (index // even) % 2
    return jnp.where(lax.axis_index("batch") % 2 == 0, (index // even) % 2, (index // odd) % 2)


def join(x, other, side):
    return jnp.where(side == 0, jnp.concatenate([x, other], axis=0), jnp.concatenate([other, x], axis=0))


def passed(x, step, counts):
    x, call = partner(x, step, counts)
    return call(x)


def down(x, step, counts):
    side = side_of(step)
    return add_low(pick(x, side, 2), passed(pick(x, 1 - side, 2), step, counts))


def parted(x, step):
    side = side_of(step)
    return pick(x, side, 2), pick(x, 1 - side, 2)


def up(x, step, counts):
    return join(x, passed(x, step, counts), side_of(step))


def up_last(x, step, counts, cuts):
    got = passed(x, step, counts)
    edges = [0, *cuts, x.shape[1]]
    return [high(join(x[:, a:b], got[:, a:b], side_of(step))) for a, b in zip(edges[:-1], edges[1:])]


def apart(certain, run):
    shapes = jax.eval_shape(run)
    return lax.cond(certain, run, lambda: jax.tree.map(lambda x: jnp.zeros(x.shape, x.dtype), shapes))


def visits(me, seq):
    short, long = (("L", me), ("R", seq - 1 - me))
    if short[1] > long[1]:
        short, long = long, short
    order = []
    for k in range(1, short[1] + 1):
        order += [(short[0], k), (long[0], k)]
    return order + [(long[0], k) for k in range(short[1] + 1, long[1] + 1)]


def choose(me, options):
    known = [(i, x) for i, x in enumerate(options) if x is not None]
    value = known[-1][1]
    for i, x in reversed(known[:-1]):
        if x is not value:
            value = jnp.where(me == i, x, value)
    return value


def pack_ids(ids, width):
    whole = jnp.zeros((8, width), jnp.bfloat16)
    both = jnp.stack([ids // ID_BASE, ids % ID_BASE]).astype(jnp.bfloat16)
    return lax.dynamic_update_slice(whole, both, (0, 0))


def unpack_ids(rows, block):
    rows = rows[:, :block].astype(jnp.int32)
    return rows[0] * ID_BASE + rows[1]


def shards(
    batch,
    seq,
    hidden_in,
    document_ids,
    query_weight,
    query_bias,
    key_weight,
    value_weight,
    value_bias,
    proj_weight,
    proj_bias,
    first_gain,
    first_shift,
    inner_weight,
    inner_bias,
    outer_weight,
    outer_bias,
    second_gain,
    second_shift,
    output_grad,
):
    hidden = hidden_in[0]
    ids = document_ids[0]
    block, width = hidden.shape
    me = lax.axis_index("seq")
    counts = {"batch": batch, "seq": seq}

    orders = [visits(i, seq) for i in range(seq)]

    came = {("L", 0): jnp.concatenate([hidden, pack_ids(ids, width)], axis=0)}
    came["R", 0] = came["L", 0]

    kv_weight = jnp.concatenate([key_weight, value_weight], axis=1)
    kv_bias = jnp.concatenate([jnp.zeros_like(value_bias), value_bias])
    queries = low(times(hidden, query_weight) + query_bias) * jnp.bfloat16(HEAD_DIM ** (-0.5))
    ids_q = ids[None, :]
    state = None
    kept = []
    for s in range(seq):
        if s < seq - 1:
            to_right = lax.ppermute(came["L", s], "seq", [(i, i + 1) for i in range(s, seq - 1)])
            to_left = lax.ppermute(came["R", s], "seq", [(i, i - 1) for i in range(1, seq - s)])
        if s == 0:
            packed, ids_k = came["L", 0], ids
        else:
            packed = choose(me, [came[orders[i][s - 1]] for i in range(seq)])
            ids_k = unpack_ids(packed[block:], block)
        tokens = hidden if s == 0 else packed[:block]
        kv = low(times(tokens, kv_weight) + kv_bias)
        state = attend_forward(queries, kv, ids_q, ids_k[:, None], state, s == seq - 1)
        if s < seq - 1:
            came["L", s + 1], came["R", s + 1], state = lax.optimization_barrier((to_right, to_left, state))
        kept.append((hidden if s == 0 else packed, kv, ids_k[:, None]))
    attended_t, totals, attended = state

    branch = times(attended, proj_weight) + proj_bias
    first, first_scaled, first_inverse = layer_norm(high(hidden) + branch, first_gain, first_shift)
    first_low = low(first)
    inner_act = times(first_low, inner_weight) + inner_bias
    chance = 0.5 * (1.0 + lax.erf(inner_act * ROOT_HALF))
    activated = low(inner_act * chance)
    slope = low(chance + inner_act * (ROOT_TAU * jnp.exp(-0.5 * inner_act * inner_act)))
    activated, slope = lax.optimization_barrier((activated, slope))
    outer_act = times(activated, outer_weight) + outer_bias
    second, second_scaled, second_inverse = layer_norm(first + outer_act, second_gain, second_shift)
    result = low(second)
    grad_mix, grad_second_gain, grad_second_shift = norm_back(
        high(output_grad[0]), second_scaled, second_inverse, second_gain
    )
    grad_outer = low(grad_mix)
    grad_outer_bias = column_sums(grad_outer)
    grad_inner = low(times_back(grad_outer, outer_weight) * high(slope))
    early = (low(weight_grad(activated, grad_outer)), low(weight_grad(first_low, grad_inner)))
    early, grad_inner = lax.optimization_barrier((early, grad_inner))
    early_sums = lax.psum(early, ("batch", "seq"))

    certain = ids[0] >= 0
    steps = steps_of(**counts)
    far = len(steps) - 1

    chips = [i for i, step in enumerate(steps) if i > 0 and step[0] == "batch"]
    places = [i for i, step in enumerate(steps) if step[0] == "seq"]

    def attention_part():
        grad_first = lax.optimization_barrier(grad_mix + times_back(grad_inner, inner_weight))
        grad_resid, grad_first_gain, grad_first_shift = norm_back(
            grad_first, first_scaled, first_inverse, first_gain
        )
        grad_branch = low(grad_resid)
        grad_attended = low(times_back(grad_branch, proj_weight))
        grad_query = None
        kv_grad = 0.0
        grad_value_bias = 0.0
        terms = {}
        for s in reversed(range(seq)):
            packed, kv, ids_k = kept[s]
            grad_kv, sums, grad_query = attend_backward(
                queries, grad_attended, kv, attended_t, totals, ids_q, ids_k, grad_query, s == 0
            )
            kv_grad += weight_grad(packed[:block], grad_kv)
            grad_value_bias += sums[0]
            terms[s] = low(times_back(grad_kv, kv_weight))
        late = jnp.concatenate(
            [low(weight_grad(hidden, grad_query)), low(kv_grad), low(weight_grad(attended, grad_branch))], axis=1
        )
        vectors = [sums[1], grad_value_bias, column_sums(grad_branch), grad_first_gain, grad_first_shift]
        own_terms = grad_resid + high(terms[0]) + times_back(grad_query, query_weight)
        return parted(down(late, steps[0], counts), steps[chips[0]]), vectors, own_terms, [terms[s] for s in range(1, seq)]

    late, sums, own_terms, terms = apart(certain, attention_part)
    terms = dict(enumerate(terms, 1))

    def homeward(s):
        found = []
        for side in "LR":
            options = [terms[orders[i].index((side, s)) + 1] if (side, s) in orders[i] else None for i in range(seq)]
            found.append(choose(me, options))
        return found

    def send(s, sends):
        return [
            lax.ppermute(sends[0], "seq", [(i, i - 1) for i in range(s, seq)]),
            lax.ppermute(sends[1], "seq", [(i, i + 1) for i in range(seq - s)]),
        ]


    def down_chips(late, vectors):
        sums = jnp.stack(
            [
                *vectors,
                grad_outer_bias,
                grad_second_gain,
                grad_second_shift,
                *jnp.split(column_sums(grad_inner), inner_weight.shape[1] // width),
            ]
        )
        sums = sums + passed(sums, steps[0], counts)
        for i in chips:
            sums = sums + passed(sums, steps[i], counts)
            if i == chips[0]:
                late = add_low(late[0], passed(late[1], steps[i], counts))
            else:
                late = down(late, steps[i], counts)
        return late, sums, {s: homeward(s) for s in range(1, seq - 1)}

    def along_row(late, sums, on_way):
        for i in places:
            sums = sums + passed(sums, steps[i], counts)
            late = down(late, steps[i], counts)
        for i in places[::-1]:
            late = up(late, steps[i], counts)
        return late, sums, [low(high(x) + high(o)) for x, o in zip(found[seq - 2], on_way)]

    late, on_way = lax.optimization_barrier((late, homeward(seq - 1)))
    on_way = send(seq - 1, on_way)
    late, sums, found = apart(certain, functools.partial(down_chips, late, sums))
    on_way, late, sums = lax.optimization_barrier((on_way, late, sums))
    late, sums, second = apart(certain, functools.partial(along_row, late, sums, on_way))
    def up_chips(late):
        for i in chips[::-1]:
            late = up(late, steps[i], counts)
        return late

    def last_part(late, early_sums):
        return up_last(late, steps[0], counts, (width, 2 * width, 3 * width)), [high(x) for x in early_sums]

    for s in reversed(range(1, seq - 1)):
        totals_home = second if s == seq - 2 else [low(high(x) + high(o)) for x, o in zip(found[s], on_way)]
        late, totals_home = lax.optimization_barrier((late, totals_home))
        on_way = send(s, totals_home)
        if s == seq - 2:
            late = apart(certain, functools.partial(up_chips, late))
            on_way, late = lax.optimization_barrier((on_way, late))
    late, early_sums = lax.optimization_barrier((late, early_sums))
    late, early_sums = apart(certain, functools.partial(last_part, late, early_sums))
    on_way, late, early_sums = lax.optimization_barrier((on_way, late, early_sums))
    vectors = sums
    grad_query_weight, grad_key_weight, grad_value_weight, grad_proj_weight = late
    grad_input = low(own_terms + high(on_way[0]) + high(on_way[1]))
    grad_outer_weight, grad_inner_weight = early_sums
    (
        grad_query_bias,
        grad_value_bias,
        grad_proj_bias,
        grad_first_gain,
        grad_first_shift,
        grad_outer_bias,
        grad_second_gain,
        grad_second_shift,
    ) = (vectors[i] for i in range(8))
    grad_inner_bias = vectors[8:].reshape(-1)
    return (
        result[None],
        grad_input[None],
        grad_query_weight,
        grad_query_bias,
        grad_key_weight,
        grad_value_weight,
        grad_value_bias,
        grad_proj_weight,
        grad_proj_bias,
        grad_first_gain,
        grad_first_shift,
        grad_inner_weight,
        grad_inner_bias,
        grad_outer_weight,
        grad_outer_bias,
        grad_second_gain,
        grad_second_shift,
    )


def solution(mesh):
    rows = P("batch", "seq", None)
    return jax.shard_map(
        functools.partial(shards, mesh.shape["batch"], mesh.shape["seq"]),
        mesh=mesh,
        in_specs=(rows, P("batch", "seq")) + (P(),) * 15 + (rows,),
        out_specs=(rows, rows) + (P(),) * 15,
        check_vma=False,
    )
```

```python
import functools

import jax
import jax.numpy as jnp
from jax import lax
from jax.experimental import pallas as pl
from jax.experimental.pallas import tpu as pltpu
from jax.sharding import PartitionSpec as P

HEAD_DIM = 64
PAIR = 2 * HEAD_DIM
MASKED = -1e30
GROUP = 2
EPSILON = 1e-05
ROOT_HALF = 0.7071067811865476
ROOT_TAU = 0.3989422804014327
ID_BASE = 128

NT = (((1,), (1,)), ((), ()))
NN = (((1,), (0,)), ((), ()))
TN = (((0,), (0,)), ((), ()))


def dot(left, right, dims):
    return lax.dot_general(left, right, dims, preferred_element_type=jnp.float32)


def low(x):
    return x.astype(jnp.bfloat16)


def high(x):
    return x.astype(jnp.float32)


def times(left, right):
    return dot(left, right, NN)


def times_back(left, right):
    return dot(left, right, NT)


def weight_grad(left, right):
    return dot(left, right, TN)


def column_sums(x):
    return jnp.sum(high(x), axis=0)


def lane_half(x, half):
    lanes = lax.broadcasted_iota(jnp.int32, x.shape, 1)
    keep = lanes < HEAD_DIM if half == 0 else lanes >= HEAD_DIM
    return jnp.where(keep, x, jnp.zeros_like(x))


def head_rows(half):
    return slice(half * HEAD_DIM, (half + 1) * HEAD_DIM)


def look(kind_ref, bias_ref, ids_q_ref, ids_k_ref):
    @pl.when(pl.program_id(0) == 0)
    def _():
        ids_q, ids_k = ids_q_ref[...], ids_k_ref[...]
        low_q, high_q, low_k, high_k = jnp.min(ids_q), jnp.max(ids_q), jnp.min(ids_k), jnp.max(ids_k)
        apart = (high_q < low_k) | (high_k < low_q)
        one = (low_q == high_k) & (low_k == high_q)
        kind_ref[0] = jnp.where(apart, 0, jnp.where(one, 1, 2)).astype(jnp.int32)

        @pl.when(kind_ref[0] == 2)
        def _():
            bias_ref[...] = jnp.where(ids_k == ids_q, 0.0, MASKED)


def forward_kernel(first, last, q_ref, k_ref, v_ref, ids_q_ref, ids_k_ref, *refs):
    if first:
        acc_in = peak_in = sum_in = None
    else:
        acc_in, peak_in, sum_in = refs[:3]
        refs = refs[3:]
    if last:
        acc_out, total_out, attended_out, acc, peak, sums, kind_ref, bias_ref = refs
    else:
        acc, peak, sums, kind_ref, bias_ref = refs
    if first:
        acc[...] = jnp.zeros_like(acc)
        sums[...] = jnp.zeros_like(sums)
        peak[...] = jnp.full(peak.shape, MASKED, jnp.float32)
    else:
        acc[...] = acc_in[...]
        sums[...] = sum_in[...]
        peak[...] = peak_in[...]
    look(kind_ref, bias_ref, ids_q_ref, ids_k_ref)

    def visit(masked):
        ones = jnp.ones((16, k_ref.shape[0]), jnp.bfloat16)
        for pair in range(GROUP):
            columns = slice(pair * PAIR, (pair + 1) * PAIR)
            q, k = q_ref[:, columns], k_ref[:, columns]
            v_t = v_ref[:, columns].T
            scores = [dot(k, lane_half(q, half), NT) for half in range(2)]
            if masked:
                scores = [x + bias_ref[...] for x in scores]
            old = [peak[pair, half : half + 1, :] for half in range(2)]
            new = [jnp.maximum(o, jnp.max(x, axis=0, keepdims=True)) for o, x in zip(old, scores)]
            prob = [low(jnp.exp(x - m)) for x, m in zip(scores, new)]
            for half in range(2):
                shrink = jnp.exp(old[half] - new[half])
                one = slice(half, half + 1)
                rows = slice(pair * PAIR + half * HEAD_DIM, pair * PAIR + (half + 1) * HEAD_DIM)
                mixed = dot(jnp.concatenate([v_t[head_rows(half)], ones], axis=0), prob[half], NN)
                acc[rows, :] = acc[rows, :] * shrink + mixed[:HEAD_DIM]
                sums[pair, one, :] = sums[pair, one, :] * shrink + mixed[HEAD_DIM : HEAD_DIM + 1]
                peak[pair, one, :] = new[half]

    pl.when(kind_ref[0] == 1)(functools.partial(visit, False))
    pl.when(kind_ref[0] == 2)(functools.partial(visit, True))

    if last:
        for pair in range(GROUP):
            for half in range(2):
                one = slice(half, half + 1)
                rows = slice(pair * PAIR + half * HEAD_DIM, pair * PAIR + (half + 1) * HEAD_DIM)
                acc_out[rows, :] = acc[rows, :] / sums[pair, one, :]
                total_out[pair, one, :] = peak[pair, one, :] + jnp.log(sums[pair, one, :])
            columns = slice(pair * PAIR, (pair + 1) * PAIR)
            attended_out[:, columns] = low(acc_out[columns, :].T)


def attend_forward(q, kv, ids_q, ids_k, state, last):
    block, width = q.shape
    pairs = width // PAIR
    first = state is None
    steps = pairs // GROUP
    rows = pl.BlockSpec((GROUP, 2, block), lambda p: (p, 0, 0))
    acc = pl.BlockSpec((GROUP * PAIR, block), lambda p: (p, 0))
    mine = pl.BlockSpec((block, GROUP * PAIR), lambda p: (0, p))
    acc_shape = jax.ShapeDtypeStruct((width, block), jnp.float32)
    row_shape = jax.ShapeDtypeStruct((pairs, 2, block), jnp.float32)
    scratch = [pltpu.SMEM((1,), jnp.int32), pltpu.VMEM((block, block), jnp.float32)]
    if last:
        out_specs = [acc, rows, mine]
        out_shape = [acc_shape, row_shape, jax.ShapeDtypeStruct((block, width), jnp.bfloat16)]
        scratch = [
            pltpu.VMEM((GROUP * PAIR, block), jnp.float32),
            pltpu.VMEM((GROUP, 2, block), jnp.float32),
            pltpu.VMEM((GROUP, 2, block), jnp.float32),
        ] + scratch
    else:
        out_specs, out_shape = [acc, rows, rows], [acc_shape, row_shape, row_shape]
    return pl.pallas_call(
        functools.partial(forward_kernel, first, last),
        grid_spec=pl.GridSpec(
            grid=(steps,),
            in_specs=[
                mine,
                mine,
                pl.BlockSpec((block, GROUP * PAIR), lambda p: (0, p + steps)),
                pl.BlockSpec((1, block), lambda p: (0, 0)),
                pl.BlockSpec((block, 1), lambda p: (0, 0)),
            ]
            + ([] if first else [acc, rows, rows]),
            out_specs=out_specs,
            scratch_shapes=scratch,
        ),
        out_shape=out_shape,
        compiler_params=pltpu.CompilerParams(vmem_limit_bytes=32 * 2**20),
        cost_estimate=pl.CostEstimate(
            flops=block, bytes_accessed=block, transcendentals=0
        ),
        name="attend_forward",
    )(q, kv, kv, ids_q, ids_k, *([] if first else state))


def backward_kernel(
    first, last, pairs, q_ref, g_ref, k_ref, v_ref, o_ref, total_ref, ids_q_ref, ids_k_ref, *refs
):
    if not first:
        grad_q_in, refs = refs[0], refs[1:]
    grad_kv, sums, grad_q_out, grad_q, kind_ref, bias_ref = refs if last else refs[:2] + (None,) + refs[2:]
    if first:
        grad_q[...] = jnp.zeros_like(grad_q)
    else:
        grad_q[...] = grad_q_in[...]
    look(kind_ref, bias_ref, ids_q_ref, ids_k_ref)
    step = pl.program_id(0)

    def columns_of(pair):
        at = step * GROUP + pair
        return pl.ds(pl.multiple_of(at * PAIR, PAIR), PAIR), pl.ds(pl.multiple_of((at + pairs) * PAIR, PAIR), PAIR)

    def visit(masked):
        for pair in range(GROUP):
            columns = slice(pair * PAIR, (pair + 1) * PAIR)
            k_columns, v_columns = columns_of(pair)
            q, g, k, v = q_ref[:, columns], g_ref[:, columns], k_ref[:, columns], v_ref[:, columns]
            k_t = k.T
            products = high(g).T * o_ref[columns, :]
            sum_k = sum_v = None
            for half in range(2):
                rows = head_rows(half)
                q_half, g_half = lane_half(q, half), lane_half(g, half)
                delta = jnp.sum(products[rows], axis=0, keepdims=True)
                scores = dot(k, q_half, NT)
                if masked:
                    scores = scores + bias_ref[...]
                prob = jnp.exp(scores - total_ref[pair, half : half + 1, :])
                grad_prob = dot(v, g_half, NT)
                grad_score = low(prob * (grad_prob - delta))
                part_v = dot(low(prob), g_half, NN)
                part_k = dot(grad_score, q_half, NN)
                sum_v = part_v if sum_v is None else sum_v + part_v
                sum_k = part_k if sum_k is None else sum_k + part_k
                mine = slice(pair * PAIR + half * HEAD_DIM, pair * PAIR + (half + 1) * HEAD_DIM)
                grad_q[mine, :] += dot(k_t[rows], grad_score, NN)
            grad_kv[:, k_columns] = low(sum_k)
            grad_kv[:, v_columns] = low(sum_v)
            sums[0:1, k_columns] = jnp.sum(high(low(sum_v)), axis=0, keepdims=True)

    pl.when(kind_ref[0] == 1)(functools.partial(visit, False))
    pl.when(kind_ref[0] == 2)(functools.partial(visit, True))

    @pl.when(kind_ref[0] == 0)
    def _():
        nothing = jnp.zeros((grad_kv.shape[0], PAIR), jnp.bfloat16)
        for pair in range(GROUP):
            k_columns, v_columns = columns_of(pair)
            grad_kv[:, k_columns] = nothing
            grad_kv[:, v_columns] = nothing
            sums[0:1, k_columns] = jnp.zeros((1, PAIR), jnp.float32)

    if last:
        for pair in range(GROUP):
            columns = slice(pair * PAIR, (pair + 1) * PAIR)
            grad_queries = low(grad_q[columns, :].T * HEAD_DIM ** (-0.5))
            grad_q_out[:, columns] = grad_queries
            sums[1:2, columns_of(pair)[0]] = jnp.sum(high(grad_queries), axis=0, keepdims=True)


def attend_backward(q, g, kv, attended_t, totals, ids_q, ids_k, grad_q, last):
    block, width = q.shape
    all_pairs = width // PAIR
    pairs = all_pairs
    steps = pairs // GROUP
    first = grad_q is None
    mine = pl.BlockSpec((block, GROUP * PAIR), lambda p: (0, p))
    acc = pl.BlockSpec((GROUP * PAIR, block), lambda p: (p, 0))
    out_specs = [
        pl.BlockSpec((block, 2 * pairs * PAIR), lambda p: (0, 0)),
        pl.BlockSpec((2, pairs * PAIR), lambda p: (0, 0)),
    ]
    out_shape = [
        jax.ShapeDtypeStruct((block, 2 * pairs * PAIR), jnp.bfloat16),
        jax.ShapeDtypeStruct((2, pairs * PAIR), jnp.float32),
    ]
    scratch = [pltpu.SMEM((1,), jnp.int32), pltpu.VMEM((block, block), jnp.float32)]
    if last:
        out_specs += [pl.BlockSpec((block, GROUP * PAIR), lambda p: (0, p))]
        out_shape += [jax.ShapeDtypeStruct((block, pairs * PAIR), jnp.bfloat16)]
        scratch = [pltpu.VMEM((GROUP * PAIR, block), jnp.float32)] + scratch
    else:
        out_specs += [acc]
        out_shape += [jax.ShapeDtypeStruct((pairs * PAIR, block), jnp.float32)]
    return pl.pallas_call(
        functools.partial(backward_kernel, first, last, pairs),
        grid_spec=pl.GridSpec(
            grid=(steps,),
            in_specs=[
                mine,
                mine,
                mine,
                pl.BlockSpec((block, GROUP * PAIR), lambda p: (0, p + steps)),
                pl.BlockSpec((GROUP * PAIR, block), lambda p: (p, 0)),
                pl.BlockSpec((GROUP, 2, block), lambda p: (p, 0, 0)),
                pl.BlockSpec((1, block), lambda p: (0, 0)),
                pl.BlockSpec((block, 1), lambda p: (0, 0)),
            ]
            + ([] if first else [acc]),
            out_specs=out_specs,
            scratch_shapes=scratch,
        ),
        out_shape=out_shape,
        compiler_params=pltpu.CompilerParams(vmem_limit_bytes=32 * 2**20),
        cost_estimate=pl.CostEstimate(
            flops=block, bytes_accessed=block, transcendentals=0
        ),
        name="attend_backward",
    )(q, g, kv, kv, attended_t, totals, ids_q, ids_k, *([] if first else [grad_q]))


def layer_norm(values, gain, shift):
    center = values - jnp.mean(values, axis=-1, keepdims=True)
    inverse = lax.rsqrt(jnp.mean(center * center, axis=-1, keepdims=True) + EPSILON)
    scaled = center * inverse
    return scaled * gain + shift, scaled, inverse


def norm_back(grad_out, scaled, inverse, gain):
    grad_scaled = grad_out * gain
    grad_in = inverse * (
        grad_scaled
        - jnp.mean(grad_scaled, axis=-1, keepdims=True)
        - scaled * jnp.mean(grad_scaled * scaled, axis=-1, keepdims=True)
    )
    return grad_in, jnp.sum(grad_out * scaled, axis=0), jnp.sum(grad_out, axis=0)


def pick(x, index, parts):
    size = x.shape[0] // parts
    return lax.dynamic_slice_in_dim(x, index * size, size, 0)


def add_low(left, right):
    return low(high(left) + high(right))


def steps_of(batch, seq):
    chips = [1 << i for i in range(1, batch.bit_length() - 1)]
    places = [1 << i for i in range(seq.bit_length() - 1)]
    return [("batch", 1, 1), *(("batch", a, b) for a, b in zip(chips, chips[::-1])), *(("seq", p, p) for p in places)]


def partner(x, step, counts):
    axis, even, odd = step
    if axis == "seq":
        paths = [(i, i ^ even) for i in range(counts["seq"])]
    else:
        paths = [(i, i ^ (odd if i % 2 else even)) for i in range(counts["batch"])]
    return x, lambda x: lax.ppermute(x, axis, paths)


def side_of(step):
    axis, even, odd = step
    index = lax.axis_index(axis)
    if even == odd:
        return (index // even) % 2
    return jnp.where(lax.axis_index("batch") % 2 == 0, (index // even) % 2, (index // odd) % 2)


def join(x, other, side):
    return jnp.where(side == 0, jnp.concatenate([x, other], axis=0), jnp.concatenate([other, x], axis=0))


def passed(x, step, counts):
    x, call = partner(x, step, counts)
    return call(x)


def down(x, step, counts):
    side = side_of(step)
    return add_low(pick(x, side, 2), passed(pick(x, 1 - side, 2), step, counts))


def parted(x, step):
    side = side_of(step)
    return pick(x, side, 2), pick(x, 1 - side, 2)


def up(x, step, counts):
    return join(x, passed(x, step, counts), side_of(step))


def up_last(x, step, counts, cuts):
    got = passed(x, step, counts)
    edges = [0, *cuts, x.shape[1]]
    return [high(join(x[:, a:b], got[:, a:b], side_of(step))) for a, b in zip(edges[:-1], edges[1:])]


def apart(certain, run):
    shapes = jax.eval_shape(run)
    return lax.cond(certain, run, lambda: jax.tree.map(lambda x: jnp.zeros(x.shape, x.dtype), shapes))


def visits(me, seq):
    short, long = (("L", me), ("R", seq - 1 - me))
    if short[1] > long[1]:
        short, long = long, short
    order = []
    for k in range(1, short[1] + 1):
        order += [(short[0], k), (long[0], k)]
    return order + [(long[0], k) for k in range(short[1] + 1, long[1] + 1)]


def choose(me, options):
    known = [(i, x) for i, x in enumerate(options) if x is not None]
    value = known[-1][1]
    for i, x in reversed(known[:-1]):
        if x is not value:
            value = jnp.where(me == i, x, value)
    return value


def pack_ids(ids, width):
    whole = jnp.zeros((8, width), jnp.bfloat16)
    both = jnp.stack([ids // ID_BASE, ids % ID_BASE]).astype(jnp.bfloat16)
    return lax.dynamic_update_slice(whole, both, (0, 0))


def unpack_ids(rows, block):
    rows = rows[:, :block].astype(jnp.int32)
    return rows[0] * ID_BASE + rows[1]


def shards(
    batch,
    seq,
    hidden_in,
    document_ids,
    query_weight,
    query_bias,
    key_weight,
    value_weight,
    value_bias,
    proj_weight,
    proj_bias,
    first_gain,
    first_shift,
    inner_weight,
    inner_bias,
    outer_weight,
    outer_bias,
    second_gain,
    second_shift,
    output_grad,
):
    hidden = hidden_in[0]
    ids = document_ids[0]
    block, width = hidden.shape
    me = lax.axis_index("seq")
    counts = {"batch": batch, "seq": seq}

    orders = [visits(i, seq) for i in range(seq)]

    came = {("L", 0): jnp.concatenate([hidden, pack_ids(ids, width)], axis=0)}
    came["R", 0] = came["L", 0]

    kv_weight = jnp.concatenate([key_weight, value_weight], axis=1)
    kv_bias = jnp.concatenate([jnp.zeros_like(value_bias), value_bias])
    queries = low(times(hidden, query_weight) + query_bias) * jnp.bfloat16(HEAD_DIM ** (-0.5))
    ids_q = ids[None, :]
    state = None
    kept = []
    for s in range(seq):
        if s < seq - 1:
            to_right = lax.ppermute(came["L", s], "seq", [(i, i + 1) for i in range(s, seq - 1)])
            to_left = lax.ppermute(came["R", s], "seq", [(i, i - 1) for i in range(1, seq - s)])
        if s == 0:
            packed, ids_k = came["L", 0], ids
        else:
            packed = choose(me, [came[orders[i][s - 1]] for i in range(seq)])
            ids_k = unpack_ids(packed[block:], block)
        tokens = hidden if s == 0 else packed[:block]
        kv = low(times(tokens, kv_weight) + kv_bias)
        state = attend_forward(queries, kv, ids_q, ids_k[:, None], state, s == seq - 1)
        if s < seq - 1:
            came["L", s + 1], came["R", s + 1], state = lax.optimization_barrier((to_right, to_left, state))
        kept.append((hidden if s == 0 else packed, kv, ids_k[:, None]))
    attended_t, totals, attended = state

    branch = times(attended, proj_weight) + proj_bias
    first, first_scaled, first_inverse = layer_norm(high(hidden) + branch, first_gain, first_shift)
    first_low = low(first)
    inner_act = times(first_low, inner_weight) + inner_bias
    chance = 0.5 * (1.0 + lax.erf(inner_act * ROOT_HALF))
    activated = low(inner_act * chance)
    slope = low(chance + inner_act * (ROOT_TAU * jnp.exp(-0.5 * inner_act * inner_act)))
    activated, slope = lax.optimization_barrier((activated, slope))
    outer_act = times(activated, outer_weight) + outer_bias
    second, second_scaled, second_inverse = layer_norm(first + outer_act, second_gain, second_shift)
    result = low(second)
    grad_mix, grad_second_gain, grad_second_shift = norm_back(
        high(output_grad[0]), second_scaled, second_inverse, second_gain
    )
    grad_outer = low(grad_mix)
    grad_outer_bias = column_sums(grad_outer)
    grad_inner = low(times_back(grad_outer, outer_weight) * high(slope))
    early = (low(weight_grad(activated, grad_outer)), low(weight_grad(first_low, grad_inner)))
    early, grad_inner = lax.optimization_barrier((early, grad_inner))
    early_sums = lax.psum(early, ("batch", "seq"))

    certain = ids[0] >= 0
    steps = steps_of(**counts)
    far = len(steps) - 1

    chips = [i for i, step in enumerate(steps) if i > 0 and step[0] == "batch"]
    places = [i for i, step in enumerate(steps) if step[0] == "seq"]

    def attention_part():
        grad_first = lax.optimization_barrier(grad_mix + times_back(grad_inner, inner_weight))
        grad_resid, grad_first_gain, grad_first_shift = norm_back(
            grad_first, first_scaled, first_inverse, first_gain
        )
        grad_branch = low(grad_resid)
        grad_attended = low(times_back(grad_branch, proj_weight))
        grad_query = None
        kv_grad = 0.0
        grad_value_bias = 0.0
        terms = {}
        for s in reversed(range(seq)):
            packed, kv, ids_k = kept[s]
            grad_kv, sums, grad_query = attend_backward(
                queries, grad_attended, kv, attended_t, totals, ids_q, ids_k, grad_query, s == 0
            )
            kv_grad += weight_grad(packed[:block], grad_kv)
            grad_value_bias += sums[0]
            terms[s] = low(times_back(grad_kv, kv_weight))
        late = jnp.concatenate(
            [low(weight_grad(hidden, grad_query)), low(kv_grad), low(weight_grad(attended, grad_branch))], axis=1
        )
        vectors = [sums[1], grad_value_bias, column_sums(grad_branch), grad_first_gain, grad_first_shift]
        own_terms = grad_resid + high(terms[0]) + times_back(grad_query, query_weight)
        return parted(down(late, steps[0], counts), steps[chips[0]]), vectors, own_terms, [terms[s] for s in range(1, seq)]

    late, sums, own_terms, terms = apart(certain, attention_part)
    terms = dict(enumerate(terms, 1))

    def homeward(s):
        found = []
        for side in "LR":
            options = [terms[orders[i].index((side, s)) + 1] if (side, s) in orders[i] else None for i in range(seq)]
            found.append(choose(me, options))
        return found

    def send(s, sends):
        return [
            lax.ppermute(sends[0], "seq", [(i, i - 1) for i in range(s, seq)]),
            lax.ppermute(sends[1], "seq", [(i, i + 1) for i in range(seq - s)]),
        ]


    def down_chips(late, vectors):
        sums = jnp.stack(
            [
                *vectors,
                grad_outer_bias,
                grad_second_gain,
                grad_second_shift,
                *jnp.split(column_sums(grad_inner), inner_weight.shape[1] // width),
            ]
        )
        sums = sums + passed(sums, steps[0], counts)
        for i in chips:
            sums = sums + passed(sums, steps[i], counts)
            if i == chips[0]:
                late = add_low(late[0], passed(late[1], steps[i], counts))
            else:
                late = down(late, steps[i], counts)
        return late, sums, {s: homeward(s) for s in range(1, seq - 1)}

    def along_row(late, sums, on_way):
        for i in places:
            sums = sums + passed(sums, steps[i], counts)
            late = down(late, steps[i], counts)
            late, sums = lax.optimization_barrier((late, sums))
        for i in places[::-1]:
            late = up(late, steps[i], counts)
        return late, sums, [low(high(x) + high(o)) for x, o in zip(found[seq - 2], on_way)]

    late, on_way = lax.optimization_barrier((late, homeward(seq - 1)))
    on_way = send(seq - 1, on_way)
    late, sums, found = apart(certain, functools.partial(down_chips, late, sums))
    on_way, late, sums = lax.optimization_barrier((on_way, late, sums))
    late, sums, second = apart(certain, functools.partial(along_row, late, sums, on_way))
    def up_chips(late):
        for i in chips[::-1]:
            late = up(late, steps[i], counts)
        return late

    def last_part(late, early_sums):
        return up_last(late, steps[0], counts, (width, 2 * width, 3 * width)), [high(x) for x in early_sums]

    for s in reversed(range(1, seq - 1)):
        totals_home = second if s == seq - 2 else [low(high(x) + high(o)) for x, o in zip(found[s], on_way)]
        late, totals_home = lax.optimization_barrier((late, totals_home))
        on_way = send(s, totals_home)
        if s == seq - 2:
            late = apart(certain, functools.partial(up_chips, late))
            on_way, late = lax.optimization_barrier((on_way, late))
    late, early_sums = lax.optimization_barrier((late, early_sums))
    late, early_sums = apart(certain, functools.partial(last_part, late, early_sums))
    on_way, late, early_sums = lax.optimization_barrier((on_way, late, early_sums))
    vectors = sums
    grad_query_weight, grad_key_weight, grad_value_weight, grad_proj_weight = late
    grad_input = low(own_terms + high(on_way[0]) + high(on_way[1]))
    grad_outer_weight, grad_inner_weight = early_sums
    (
        grad_query_bias,
        grad_value_bias,
        grad_proj_bias,
        grad_first_gain,
        grad_first_shift,
        grad_outer_bias,
        grad_second_gain,
        grad_second_shift,
    ) = (vectors[i] for i in range(8))
    grad_inner_bias = vectors[8:].reshape(-1)
    return (
        result[None],
        grad_input[None],
        grad_query_weight,
        grad_query_bias,
        grad_key_weight,
        grad_value_weight,
        grad_value_bias,
        grad_proj_weight,
        grad_proj_bias,
        grad_first_gain,
        grad_first_shift,
        grad_inner_weight,
        grad_inner_bias,
        grad_outer_weight,
        grad_outer_bias,
        grad_second_gain,
        grad_second_shift,
    )


def solution(mesh):
    rows = P("batch", "seq", None)
    return jax.shard_map(
        functools.partial(shards, mesh.shape["batch"], mesh.shape["seq"]),
        mesh=mesh,
        in_specs=(rows, P("batch", "seq")) + (P(),) * 15 + (rows,),
        out_specs=(rows, rows) + (P(),) * 15,
        check_vma=False,
    )
```
